512 devices in a mesh: sub: 32 (over z_lo, x, core), freq: 16 (over z_hi, y).
Axes of the slice: x: 4, y: 4, z: 16 (z_hi: 4, z_lo: 4; z = z_hi * 4 + z_lo), core: 2. Of those that a mesh axis runs over, the one named last changes fastest.
Arguments:
- right_side: float32 [16384, 16, 2, 128], P('sub', 'freq'), may hold values from -56 to 56
- schur: bfloat16 [16, 2, 16384, 512], P('freq', None, 'sub'), may hold values from -0.5 to 3.5
- match_blocks: int32 [32, 3], P('sub'), may hold values from 0 to 3
Outputs:
- response: float32 [16, 16384, 128], P('freq', 'sub')
The draws below stay inside these ranges and needn't reach their ends.
All inputs are finite; a program needn't handle non-finite values.
Results may differ from the reference program's by a relative error of at most 0.0024.
Values may be sent and summed in bfloat16 or wider, within the bound.
A program may use at most 64 MiB of HBM per device.

```python
import math
import jax
import jax.numpy as jnp
from jax import lax

NI = 512
BLOCK = 128
LOADS = 128
ITERS = 3
ROUNDS = 3
SUBS = 32
FREQS = 16
NT = 16
NB = 4
N_SUB = 32


def draw_right_side(key, part):
    key = jax.random.fold_in(key, 11)
    first, second, third = jax.random.split(key, 3)
    shape = (SUBS * NI, FREQS, 2, LOADS)
    rows = jnp.arange(SUBS * NI)
    owner = rows // NI
    rise = jnp.exp(math.log(3.0) * (owner.astype(jnp.float32) / (SUBS - 1) - 0.5))
    row_scale = jnp.exp(jax.random.uniform(second, (SUBS * NI,), minval=math.log(0.5), maxval=math.log(2.0))) * rise
    load_weight = jnp.exp(jax.random.uniform(third, (SUBS, LOADS), minval=math.log(0.25), maxval=math.log(4.0)))
    row_weight = jnp.take(load_weight, owner, axis=0)
    base = jnp.clip(jax.random.normal(first, shape), -4.0, 4.0)
    return (base * row_scale[:, None, None, None] * row_weight[:, None, None, :]).astype(jnp.float32)


def draw_schur(key, part):
    key = jax.random.fold_in(key, 23)
    first, second, third, fourth, fifth = jax.random.split(key, 5)
    shape = (FREQS, 2, SUBS * NI, NI)
    owner = jnp.arange(SUBS * NI) // NI
    trend = owner.astype(jnp.float32) / (SUBS - 1)
    offdiag = jnp.clip(jax.random.normal(first, shape), -4.0, 4.0) * (0.6 / math.sqrt(NI))
    jitter_real = jax.random.uniform(fourth, (FREQS, SUBS), minval=0.0, maxval=0.5)
    level_imag = jax.random.uniform(fifth, (FREQS, SUBS), minval=0.2, maxval=0.8)
    diag_real = 1.1 + trend[None, :] + jnp.take(jitter_real, owner, axis=1) + jax.random.uniform(second, (FREQS, SUBS * NI), minval=0.0, maxval=0.3)
    diag_imag = jnp.take(level_imag, owner, axis=1) + jax.random.uniform(third, (FREQS, SUBS * NI), minval=0.0, maxval=0.3)
    identity = ((jnp.arange(SUBS * NI) % NI)[:, None] == jnp.arange(NI)[None, :]).astype(jnp.float32)
    diagonal = jnp.stack([diag_real, diag_imag], axis=1)[:, :, :, None] * identity[None, None]
    return (offdiag + diagonal).astype(jnp.bfloat16)


def place_ends(values, rng, least, top_value):
    dims = values.shape
    spot = [jax.random.randint(jax.random.fold_in(rng, axis), (), 0, dims[axis]) for axis in range(len(dims))]
    values = values.at[tuple(spot)].set(least)
    longest = dims.index(max(dims))
    spot[longest] = (spot[longest] + 1) % dims[longest]
    return values.at[tuple(spot)].set(top_value)


def setup_inputs(seed: int = 0) -> dict:
    key_list = jax.random.split(jax.random.key(seed), 4)
    return {
        "right_side": draw_right_side(jax.random.fold_in(key_list[3], 71), 0),
        "schur": draw_schur(jax.random.fold_in(key_list[3], 71), 0),
        "match_blocks": place_ends(jax.random.randint(key_list[2], (SUBS, ROUNDS), 0, NB), jax.random.fold_in(key_list[2], 1), 0, NB - 1).astype(jnp.int32),
    }


KAPPA = 0.5
DECAY = 0.5
EPS = 1e-06

def phase_table(times, freqs, total_times, total_freqs):
    level = (2 * freqs[None, :] + 1) * times[:, None] % (2 * total_times)
    angle = jnp.pi * level.astype(jnp.float32) / total_times
    damp = jnp.exp(DECAY * times.astype(jnp.float32) / total_times) / jnp.sqrt(jnp.float32(total_freqs))
    return jnp.stack([jnp.cos(angle), -jnp.sin(angle)], axis=2) * damp[:, None, None]

def reference(right_side, schur, match_blocks):
    logs = N_SUB.bit_length() - 1
    subs = N_SUB
    nblk = NI // BLOCK
    high = lax.Precision.HIGHEST
    blocks = schur.reshape(FREQS, 2, subs, NI, NI)
    ids = jnp.arange(subs, dtype=jnp.int32)

    def apply(q):
        qf = q.astype(jnp.float32)

        def one(args):
            sf, qq = args
            sf = sf.astype(jnp.float32)
            real = jnp.einsum('sij,sjl->sil', sf[0], qq[:, :, 0], precision=high) - jnp.einsum('sij,sjl->sil', sf[1], qq[:, :, 1], precision=high)
            imag = jnp.einsum('sij,sjl->sil', sf[0], qq[:, :, 1], precision=high) + jnp.einsum('sij,sjl->sil', sf[1], qq[:, :, 0], precision=high)
            return jnp.stack([real, imag], axis=2)
        prod = lax.map(one, (blocks, jnp.moveaxis(qf, 2, 0)))
        prod = jnp.moveaxis(prod, 0, 2)
        qb = qf.reshape(subs, nblk, BLOCK, FREQS, 2, LOADS)
        couple = jnp.zeros(qb.shape, jnp.float32)
        for rnd in range(ROUNDS):
            bit = rnd * logs // ROUNDS
            partner = ids ^ 1 << bit
            source = qb[partner, match_blocks[partner, rnd]]
            couple = couple.at[ids, match_blocks[:, rnd]].add(source)
        return prod - KAPPA * couple.reshape(prod.shape)
    res = right_side.reshape(subs, NI, FREQS, 2, LOADS)
    sol_re = jnp.zeros(res[:, :, :, 0].shape, jnp.float32)
    sol_im = jnp.zeros(res[:, :, :, 0].shape, jnp.float32)
    for step in range(ITERS):
        q = res.astype(jnp.bfloat16)
        image = apply(q)
        w_re, w_im = (image[:, :, :, 0], image[:, :, :, 1])
        r_re, r_im = (res[:, :, :, 0], res[:, :, :, 1])
        num_re = lax.optimization_barrier(jnp.sum(w_re * r_re + w_im * r_im, axis=(0, 1)))
        num_im = lax.optimization_barrier(jnp.sum(w_re * r_im - w_im * r_re, axis=(0, 1)))
        den = lax.optimization_barrier(jnp.sum(w_re * w_re + w_im * w_im, axis=(0, 1))) + EPS
        a_re = num_re / den
        a_im = num_im / den
        sol_re = sol_re + a_re * r_re - a_im * r_im
        sol_im = sol_im + a_re * r_im + a_im * r_re
        new_re = r_re - (a_re * w_re - a_im * w_im)
        new_im = r_im - (a_re * w_im + a_im * w_re)
        res = jnp.stack([new_re, new_im], axis=3)
    solution = jnp.stack([sol_re, sol_im], axis=3).reshape(subs * NI, FREQS, 2, LOADS)
    table = phase_table(jnp.arange(NT, dtype=jnp.int32), jnp.arange(FREQS, dtype=jnp.int32), NT, FREQS)
    return jnp.einsum('kfc,ifcl->kil', table, solution, precision=high)
```

```python
import jax
import jax.numpy as jnp
import numpy as np
from jax import lax
from jax.experimental import pallas as pl
from jax.experimental.pallas import tpu as pltpu
from jax.sharding import PartitionSpec as P

MESH = pl.DeviceIdType.MESH
F32 = jnp.float32
BF16 = jnp.bfloat16

BLOCK = 128
KAPPA = 0.5
DECAY = 0.5
EPS = 1e-06
ROUNDS = 3
NY = 4
CH = 32


def phase_table(count):
    times = np.arange(count)
    freqs = np.arange(count)
    level = (2 * freqs[None, :] + 1) * times[:, None] % (2 * count)
    angle = np.pi * level / count
    damp = np.exp(DECAY * times / count) / np.sqrt(count)
    table = np.stack([np.cos(angle), -np.sin(angle)], axis=2) * damp[:, None, None]
    return table.astype(np.float32).reshape(-1)


def cmul(a, b):
    return (a[0] * b[0] - a[1] * b[1], a[0] * b[1] + a[1] * b[0])


def conj(a):
    return (a[0], -a[1])


def cadd(a, b):
    return (a[0] + b[0], a[1] + b[1])


def csub(a, b):
    return (a[0] - b[0], a[1] - b[1])


def scale(r, a):
    return (r * a[0], r * a[1])


def abs2(a):
    return a[0] * a[0] + a[1] * a[1]


def divide(a, d):
    return (a[0] / d, a[1] / d)


def combination(g):
    g10, g11, g20, g21, g22, g30, g31, g32, g33 = g
    a0 = divide(g10, g11 + EPS)
    n1 = csub(g10, scale(g11, a0))
    n1 = csub(n1, cmul(conj(a0), g20))
    n1 = cadd(n1, scale(abs2(a0), g21))
    d1 = g11 - 2.0 * cmul(a0, conj(g21))[0] + abs2(a0) * g22
    a1 = divide(n1, jnp.maximum(d1, 0.0) + EPS)
    b = cadd(a0, a1)
    d = cmul(a0, a1)
    n2 = cadd(csub(g10, scale(g11, b)), cmul(d, conj(g21)))
    t = cadd(csub(g20, cmul(b, g21)), scale(g22, d))
    n2 = csub(n2, cmul(conj(b), t))
    t = cadd(csub(g30, cmul(b, g31)), cmul(d, g32))
    n2 = cadd(n2, cmul(conj(d), t))
    d2 = g11 + abs2(b) * g22 + abs2(d) * g33
    d2 = d2 - 2.0 * cmul(b, conj(g21))[0] + 2.0 * cmul(d, conj(g31))[0]
    d2 = d2 - 2.0 * cmul(cmul(conj(b), d), conj(g32))[0]
    a2 = divide(n2, jnp.maximum(d2, 0.0) + EPS)
    w0 = cadd(b, a2)
    w1 = scale(-1.0, cadd(d, cmul(a2, b)))
    wu = scale(-1.0, cmul(a2, a1))
    w2 = cmul(d, a2)
    return w0, w1, wu, w2


def kernel(
    mb_hbm, tbl_hbm, rs_hbm, sch_hbm, out_ref,
    mb, tbl, rs, sch, v0, v1, v2, u1, q, qlo, prod,
    ex_send, ex_recv, ga_send, ga_recv, gb_send, gb_recv,
    z1s, z1r, y1s, y1r, own, p2s, p2r, keep, z3s, z3r, y3s, y3r,
    in_sem, ex_ss, ex_rs, ga_ss, ga_rs, gb_ss, gb_rs,
    z1_ss, z1_rs, y1_ss, y1_rs, p2_ss, p2_rs, z3_ss, z3_rs, y3_ss, y3_rs,
):
    s = lax.axis_index("sub")
    f = lax.axis_index("freq")
    nsub = lax.axis_size("sub")
    z, y = f // NY, f % NY
    ni = v0.shape[0]
    nb = ni // BLOCK
    load = v0.shape[1] // 2

    def flip(bit):
        return s + bit - 2 * bit * ((s // bit) % 2)

    partners = [flip(1), flip(2), flip(8)]
    group = [(s // 8) * 8 + (s + off) % 8 for off in range(1, 8)]
    layers = [(s + 8 * off) % nsub for off in range(1, 4)]
    ze = z + 1 - 2 * (z % 2)
    zo = 3 - z
    opp = 3 - ze
    za = (ze, zo)

    def yt(off):
        return (y + off) % NY

    def yf(off):
        return (y + NY - off) % NY

    sends = []

    def send(src, dst, ss, rsem, sub, freq):
        copy = pltpu.make_async_remote_copy(
            src_ref=src, dst_ref=dst, send_sem=ss, recv_sem=rsem,
            device_id={"sub": sub, "freq": freq}, device_id_type=MESH,
        )
        copy.start()
        sends.append(copy)
        return copy

    c_mb = pltpu.make_async_copy(mb_hbm, mb, in_sem.at[0])
    c_tbl = pltpu.make_async_copy(tbl_hbm, tbl, in_sem.at[1])
    c_rs = pltpu.make_async_copy(rs_hbm, rs, in_sem.at[2])
    c_sch = pltpu.make_async_copy(sch_hbm, sch, in_sem.at[3])
    c_rs.start()
    c_mb.start()
    c_sch.start()
    c_tbl.start()

    barrier = pltpu.get_barrier_semaphore()
    peers = [(p, f) for p in group + layers]
    peers += [(s, z * NY + yt(off)) for off in range(1, NY)]
    peers += [(s, zt * NY + yt(off)) for zt in za for off in range(NY)]
    for ps, pf in peers:
        pl.semaphore_signal(barrier, inc=1, device_id={"sub": ps, "freq": pf}, device_id_type=MESH)

    c_rs.wait()
    for k in range(nb):
        for c in range(2):
            part = rs[pl.ds(2 * BLOCK * k + c, BLOCK, stride=2), :]
            rows, cols = pl.ds(k * BLOCK, BLOCK), pl.ds(c * load, load)
            v0[rows, cols] = part
            high = part.astype(BF16)
            q[rows, cols] = high
            qlo[rows, cols] = (part - high.astype(F32)).astype(BF16)
    c_mb.wait()
    pl.semaphore_wait(barrier, len(peers))

    def match(r, k):
        gap = (mb[0, r] - k).astype(F32)
        return jnp.maximum(1.0 - gap * gap, 0.0)

    def exchange(j):
        out = []
        for r in (1, 2, 0):
            block = None
            for k in range(nb):
                part = match(r, k) * q[pl.ds(k * BLOCK, BLOCK), :].astype(F32)
                block = part if block is None else block + part
            ex_send[j, r] = block.astype(BF16)
            out.append(send(ex_send.at[j, r], ex_recv.at[j, r], ex_ss.at[j, r], ex_rs.at[j, r], partners[r], f))
        return out

    def image(j, k):
        top = prod[pl.ds(k * BLOCK, BLOCK), :]
        low = prod[pl.ds(ni + k * BLOCK, BLOCK), :]
        re = top[:, :load] - low[:, load:]
        im = top[:, load:] + low[:, :load]
        if j is not None:
            for r in range(ROUNDS):
                weight = KAPPA * match(r, k)
                inc = ex_recv[j, r].astype(F32)
                re = re - weight * inc[:, :load]
                im = im - weight * inc[:, load:]
        return re, im

    def fold(a):
        return jnp.sum(a.reshape(BLOCK // 8, 8, load), axis=0)

    def pair(v, k):
        rows = pl.ds(k * BLOCK, BLOCK)
        return v[rows, :load], v[rows, load:]

    def inner(a, b):
        return [fold(a[0] * b[0] + a[1] * b[1]), fold(a[0] * b[1] - a[1] * b[0])]

    def total(parts):
        acc = parts[0]
        for p in parts[1:]:
            acc = [i + j for i, j in zip(acc, p)]
        return [jnp.sum(a, axis=0, keepdims=True) for a in acc]

    moves = exchange(0)
    c_sch.wait()
    prod[...] = jnp.dot(sch[...], qlo[...], preferred_element_type=F32)
    for k in range(nb):
        re, im = image(None, k)
        rows = pl.ds(k * BLOCK, BLOCK)
        u1[rows, :load] = re
        u1[rows, load:] = im
    prod[...] = jnp.dot(sch[...], q[...], preferred_element_type=F32)
    for m in moves:
        m.wait_recv()
    for k in range(nb):
        re, im = image(0, k)
        rows = pl.ds(k * BLOCK, BLOCK)
        v1[rows, :load] = re
        v1[rows, load:] = im
        q[rows, :load] = re.astype(BF16)
        q[rows, load:] = im.astype(BF16)
    moves = exchange(1)
    for k in range(nb):
        rows = pl.ds(k * BLOCK, BLOCK)
        qlo[rows, :] = (v1[rows, :] - q[rows, :].astype(F32)).astype(BF16)
    prod[...] = jnp.dot(sch[...], q[...], preferred_element_type=F32) + jnp.dot(
        sch[...], qlo[...], preferred_element_type=F32
    )
    rows1 = []
    for k in range(nb):
        a = pair(v1, k)
        rows1.append(inner(a, pair(v0, k)) + [fold(abs2(a))])
    rows1 = total(rows1)
    for m in moves:
        m.wait_recv()
    for k in range(nb):
        re, im = image(1, k)
        rows = pl.ds(k * BLOCK, BLOCK)
        v2[rows, :load] = re
        v2[rows, load:] = im
        q[rows, :load] = re.astype(BF16)
        q[rows, load:] = im.astype(BF16)
    moves = exchange(2)
    prod[...] = jnp.dot(sch[...], q[...], preferred_element_type=F32)
    rows2 = []
    for k in range(nb):
        a = pair(v2, k)
        rows2.append(inner(a, pair(v0, k)) + inner(a, pair(v1, k)) + [fold(abs2(a))])
    rows2 = total(rows2)
    for m in moves:
        m.wait_recv()
    rows3 = []
    for k in range(nb):
        a = image(2, k)
        rows3.append(
            inner(a, pair(v0, k)) + inner(a, pair(v1, k)) + inner(a, pair(v2, k)) + [fold(abs2(a))]
        )
    rows3 = total(rows3)

    for i, row in enumerate(rows1 + rows2 + rows3):
        ga_send[i : i + 1, :] = row
    ga_send[15:16, :] = jnp.zeros((1, load), F32)
    moves = [
        send(ga_send, ga_recv.at[i], ga_ss.at[i], ga_rs.at[i], p, f) for i, p in enumerate(group)
    ]
    acc = ga_send[...]
    for i, m in enumerate(moves):
        m.wait_recv()
        acc = acc + ga_recv[i]
    gb_send[...] = acc
    moves = [
        send(gb_send, gb_recv.at[i], gb_ss.at[i], gb_rs.at[i], p, f) for i, p in enumerate(layers)
    ]
    for i, m in enumerate(moves):
        m.wait_recv()
        acc = acc + gb_recv[i]
    row = [acc[i : i + 1, :] for i in range(15)]
    weights = combination((
        (row[0], row[1]), row[2], (row[3], row[4]), (row[5], row[6]), row[7],
        (row[8], row[9]), (row[10], row[11]), (row[12], row[13]), row[14],
    ))
    basis = (v0, v1, u1, v2)

    def solved(start):
        rows = pl.ds(pl.multiple_of(start, CH), CH)
        re = im = None
        for (wr, wi), v in zip(weights, basis):
            a, b = v[rows, :load], v[rows, load:]
            tr, ti = wr * a - wi * b, wr * b + wi * a
            re, im = (tr, ti) if re is None else (re + tr, im + ti)
        return re, im

    def place(half, zt, yt_):
        if half == 0:
            return yt_ * (4 * CH) + (((zt + 1) // 2) % 2) * CH
        return yt_ * (4 * CH) + 2 * CH + (zt // 2) * CH

    z_moves, y_moves = [[], []], [[], []]
    for off in range(NY):
        for h in range(2):
            re, im = solved(place(h, za[h], yt(off)))
            z1s[h, off, :, :load] = re.astype(BF16)
            z1s[h, off, :, load:] = im.astype(BF16)
            z_moves[h].append(
                send(z1s.at[h, off], z1r.at[h, off], z1_ss.at[h, off], z1_rs.at[h, off], s, za[h] * NY + yt(off))
            )
    for off in range(1, NY):
        for h in range(2):
            re, im = solved(place(h, z, yt(off)))
            y1s[h, off - 1, :, :load] = re
            y1s[h, off - 1, :, load:] = im
            y_moves[h].append(
                send(y1s.at[h, off - 1], y1r.at[h, off - 1], y1_ss.at[h, off - 1], y1_rs.at[h, off - 1], s, z * NY + yt(off))
            )
    for h in range(2):
        re, im = solved(place(h, z, y))
        own[h, :, :load] = re
        own[h, :, load:] = im
    c_tbl.wait()

    def sources(h):
        out = [(z * NY + y, own.at[h])]
        out += [(z * NY + yf(off), y1r.at[h, off - 1]) for off in range(1, NY)]
        out += [(za[h] * NY + yf(off), z1r.at[h, off]) for off in range(NY)]
        return out

    def combine(h, zt):
        acc = [None] * NY
        for fs, ref in sources(h):
            re, im = ref[:, :load].astype(F32), ref[:, load:].astype(F32)
            for off in range(NY):
                at = ((zt * NY + yt(off)) * (4 * NY) + fs) * 2
                term = tbl[at] * re + tbl[at + 1] * im
                acc[off] = term if acc[off] is None else acc[off] + term
        return acc

    p_moves = [[], []]
    for h in range(2):
        for m in z_moves[h] + y_moves[h]:
            m.wait_recv()
        for slot, zt in enumerate((za[1 - h], opp)):
            acc = combine(h, zt)
            for off in range(NY):
                p2s[h, slot, off] = acc[off].astype(BF16)
            p_moves[h].append(
                send(p2s.at[h, slot], p2r.at[h, slot], p2_ss.at[h, slot], p2_rs.at[h, slot], s, za[1 - h] * NY + y)
            )
    for h in range(2):
        for slot, zt in ((1, za[h]), (0, z)):
            acc = combine(h, zt)
            for off in range(NY):
                keep[h, slot, off] = acc[off]

    z_moves, y_moves = [[], []], [[], []]
    for h in range(2):
        p_moves[h][1].wait_recv()
        for off in range(NY):
            z3s[h, off] = (keep[h, 1, off] + p2r[h, 1, off].astype(F32)).astype(BF16)
            z_moves[h].append(
                send(z3s.at[h, off], z3r.at[h, off], z3_ss.at[h, off], z3_rs.at[h, off], s, za[h] * NY + yt(off))
            )
    for h in range(2):
        p_moves[h][0].wait_recv()
        for off in range(1, NY):
            y3s[h, off - 1] = keep[h, 0, off] + p2r[h, 0, off].astype(F32)
            y_moves[h].append(
                send(y3s.at[h, off - 1], y3r.at[h, off - 1], y3_ss.at[h, off - 1], y3_rs.at[h, off - 1], s, z * NY + yt(off))
            )
        rows = pl.ds(pl.multiple_of(place(h, z, y), CH), CH)
        out_ref[rows, :] = keep[h, 0, 0] + p2r[h, 0, 0].astype(F32)
    for h in range(2):
        for off in range(1, NY):
            y_moves[h][off - 1].wait_recv()
            rows = pl.ds(pl.multiple_of(place(h, z, yf(off)), CH), CH)
            out_ref[rows, :] = y3r[h, off - 1]
    for h in range(2):
        for off in range(NY):
            z_moves[h][off].wait_recv()
            rows = pl.ds(pl.multiple_of(place(h, za[h], yf(off)), CH), CH)
            out_ref[rows, :] = z3r[h, off].astype(F32)
    for m in sends:
        m.wait_send()


def shards(right_side, schur, match_blocks):
    ni, _, _, loads = right_side.shape
    freqs = lax.axis_size("freq")
    wide = 2 * loads
    dma = pltpu.SemaphoreType.DMA
    vmem = pltpu.VMEM
    out = pl.pallas_call(
        kernel,
        out_shape=jax.ShapeDtypeStruct((ni, loads), F32),
        in_specs=[pl.BlockSpec(memory_space=pl.ANY)] * 4,
        out_specs=pl.BlockSpec(memory_space=pltpu.VMEM),
        scratch_shapes=[
            pltpu.SMEM((1, ROUNDS), jnp.int32),
            pltpu.SMEM((2 * freqs * freqs,), F32),
            vmem((2 * ni, loads), F32),
            vmem((2 * ni, ni), BF16),
            vmem((ni, wide), F32),
            vmem((ni, wide), F32),
            vmem((ni, wide), F32),
            vmem((ni, wide), F32),
            vmem((ni, wide), BF16),
            vmem((ni, wide), BF16),
            vmem((2 * ni, wide), F32),
            vmem((3, ROUNDS, BLOCK, wide), BF16),
            vmem((3, ROUNDS, BLOCK, wide), BF16),
            vmem((16, loads), F32),
            vmem((7, 16, loads), F32),
            vmem((16, loads), F32),
            vmem((3, 16, loads), F32),
            vmem((2, NY, CH, wide), BF16),
            vmem((2, NY, CH, wide), BF16),
            vmem((2, NY - 1, CH, wide), F32),
            vmem((2, NY - 1, CH, wide), F32),
            vmem((2, CH, wide), F32),
            vmem((2, 2, NY, CH, loads), BF16),
            vmem((2, 2, NY, CH, loads), BF16),
            vmem((2, 2, NY, CH, loads), F32),
            vmem((2, NY, CH, loads), BF16),
            vmem((2, NY, CH, loads), BF16),
            vmem((2, NY - 1, CH, loads), F32),
            vmem((2, NY - 1, CH, loads), F32),
            dma((4,)),
            dma((3, ROUNDS)), dma((3, ROUNDS)),
            dma((7,)), dma((7,)),
            dma((3,)), dma((3,)),
            dma((2, NY)), dma((2, NY)),
            dma((2, NY - 1)), dma((2, NY - 1)),
            dma((2, 2)), dma((2, 2)),
            dma((2, NY)), dma((2, NY)),
            dma((2, NY - 1)), dma((2, NY - 1)),
        ],
        compiler_params=pltpu.CompilerParams(
            collective_id=0, has_side_effects=True, vmem_limit_bytes=32 * 1024 * 1024
        ),
    )(
        match_blocks,
        jnp.asarray(phase_table(freqs)),
        right_side.reshape(2 * ni, loads),
        schur.reshape(2 * ni, ni),
    )
    return out.reshape(1, ni, loads)


def solution(mesh):
    return jax.shard_map(
        shards,
        mesh=mesh,
        in_specs=(P("sub", "freq", None, None), P("freq", None, "sub", None), P("sub", None)),
        out_specs=P("freq", "sub", None),
        check_vma=False,
    )
```

```python
import jax
import jax.numpy as jnp
import numpy as np
from jax import lax
from jax.experimental import pallas as pl
from jax.experimental.pallas import tpu as pltpu
from jax.sharding import PartitionSpec as P

MESH = pl.DeviceIdType.MESH
F32 = jnp.float32
BF16 = jnp.bfloat16

BLOCK = 128
KAPPA = 0.5
DECAY = 0.5
EPS = 1e-06
ROUNDS = 3
NY = 4
CH = 32


def phase_table(count):
    times = np.arange(count)
    freqs = np.arange(count)
    level = (2 * freqs[None, :] + 1) * times[:, None] % (2 * count)
    angle = np.pi * level / count
    damp = np.exp(DECAY * times / count) / np.sqrt(count)
    table = np.stack([np.cos(angle), -np.sin(angle)], axis=2) * damp[:, None, None]
    return table.astype(np.float32).reshape(-1)


def cmul(a, b):
    return (a[0] * b[0] - a[1] * b[1], a[0] * b[1] + a[1] * b[0])


def conj(a):
    return (a[0], -a[1])


def cadd(a, b):
    return (a[0] + b[0], a[1] + b[1])


def csub(a, b):
    return (a[0] - b[0], a[1] - b[1])


def scale(r, a):
    return (r * a[0], r * a[1])


def abs2(a):
    return a[0] * a[0] + a[1] * a[1]


def divide(a, d):
    return (a[0] / d, a[1] / d)


def combination(g):
    g10, g11, g20, g21, g22, g30, g31, g32, g33 = g
    a0 = divide(g10, g11 + EPS)
    n1 = csub(g10, scale(g11, a0))
    n1 = csub(n1, cmul(conj(a0), g20))
    n1 = cadd(n1, scale(abs2(a0), g21))
    d1 = g11 - 2.0 * cmul(a0, conj(g21))[0] + abs2(a0) * g22
    a1 = divide(n1, jnp.maximum(d1, 0.0) + EPS)
    b = cadd(a0, a1)
    d = cmul(a0, a1)
    n2 = cadd(csub(g10, scale(g11, b)), cmul(d, conj(g21)))
    t = cadd(csub(g20, cmul(b, g21)), scale(g22, d))
    n2 = csub(n2, cmul(conj(b), t))
    t = cadd(csub(g30, cmul(b, g31)), cmul(d, g32))
    n2 = cadd(n2, cmul(conj(d), t))
    d2 = g11 + abs2(b) * g22 + abs2(d) * g33
    d2 = d2 - 2.0 * cmul(b, conj(g21))[0] + 2.0 * cmul(d, conj(g31))[0]
    d2 = d2 - 2.0 * cmul(cmul(conj(b), d), conj(g32))[0]
    a2 = divide(n2, jnp.maximum(d2, 0.0) + EPS)
    w0 = cadd(b, a2)
    w1 = scale(-1.0, cadd(d, cmul(a2, b)))
    wu = scale(-1.0, cmul(a2, a1))
    w2 = cmul(d, a2)
    return w0, w1, wu, w2


def kernel(
    mb_hbm, tbl_hbm, rs_hbm, sch_hbm, out_ref,
    mb, tbl, rs, sch, v0, v1, v2, u1, q, qlo, prod,
    ex_send, ex_recv, ga_send, ga_recv, gb_send, gb_recv,
    z1s, z1r, y1s, y1r, own, p2s, p2r, keep, z3s, z3r, y3s, y3r,
    in_sem, ex_ss, ex_rs, ga_ss, ga_rs, gb_ss, gb_rs,
    z1_ss, z1_rs, y1_ss, y1_rs, p2_ss, p2_rs, z3_ss, z3_rs, y3_ss, y3_rs,
):
    s = lax.axis_index("sub")
    f = lax.axis_index("freq")
    nsub = lax.axis_size("sub")
    z, y = f // NY, f % NY
    ni = v0.shape[0]
    nb = ni // BLOCK
    load = v0.shape[1] // 2

    def flip(bit):
        return s + bit - 2 * bit * ((s // bit) % 2)

    partners = [flip(1), flip(2), flip(8)]
    group = [(s // 8) * 8 + (s + off) % 8 for off in range(1, 8)]
    layers = [(s + 8 * off) % nsub for off in range(1, 4)]
    ze = z + 1 - 2 * (z % 2)
    zo = 3 - z
    opp = 3 - ze
    za = (ze, zo)

    def yt(off):
        return (y + off) % NY

    def yf(off):
        return (y + NY - off) % NY

    sends = []

    def send(src, dst, ss, rsem, sub, freq):
        copy = pltpu.make_async_remote_copy(
            src_ref=src, dst_ref=dst, send_sem=ss, recv_sem=rsem,
            device_id={"sub": sub, "freq": freq}, device_id_type=MESH,
        )
        copy.start()
        sends.append(copy)
        return copy

    c_mb = pltpu.make_async_copy(mb_hbm, mb, in_sem.at[0])
    c_tbl = pltpu.make_async_copy(tbl_hbm, tbl, in_sem.at[1])
    c_rs = pltpu.make_async_copy(rs_hbm, rs, in_sem.at[2])
    c_sch = pltpu.make_async_copy(sch_hbm, sch, in_sem.at[3])
    c_rs.start()
    c_mb.start()
    c_sch.start()
    c_tbl.start()

    barrier = pltpu.get_barrier_semaphore()
    peers = [(p, f) for p in group + layers]
    peers += [(s, z * NY + yt(off)) for off in range(1, NY)]
    peers += [(s, zt * NY + yt(off)) for zt in za for off in range(NY)]
    for ps, pf in peers:
        pl.semaphore_signal(barrier, inc=1, device_id={"sub": ps, "freq": pf}, device_id_type=MESH)

    c_rs.wait()
    for k in range(nb):
        for c in range(2):
            part = rs[pl.ds(2 * BLOCK * k + c, BLOCK, stride=2), :]
            rows, cols = pl.ds(k * BLOCK, BLOCK), pl.ds(c * load, load)
            v0[rows, cols] = part
            high = part.astype(BF16)
            q[rows, cols] = high
            qlo[rows, cols] = (part - high.astype(F32)).astype(BF16)
    c_mb.wait()
    pl.semaphore_wait(barrier, len(peers))

    def match(r, k):
        gap = (mb[0, r] - k).astype(F32)
        return jnp.maximum(1.0 - gap * gap, 0.0)

    def exchange(j):
        out = []
        for r in (1, 2, 0):
            block = None
            for k in range(nb):
                part = match(r, k) * q[pl.ds(k * BLOCK, BLOCK), :].astype(F32)
                block = part if block is None else block + part
            ex_send[j, r] = block.astype(BF16)
            out.append(send(ex_send.at[j, r], ex_recv.at[j, r], ex_ss.at[j, r], ex_rs.at[j, r], partners[r], f))
        return out

    def image(j, k):
        top = prod[pl.ds(k * BLOCK, BLOCK), :]
        low = prod[pl.ds(ni + k * BLOCK, BLOCK), :]
        re = top[:, :load] - low[:, load:]
        im = top[:, load:] + low[:, :load]
        if j is not None:
            for r in range(ROUNDS):
                weight = KAPPA * match(r, k)
                inc = ex_recv[j, r].astype(F32)
                re = re - weight * inc[:, :load]
                im = im - weight * inc[:, load:]
        return re, im

    def fold(a):
        return jnp.sum(a.reshape(BLOCK // 8, 8, load), axis=0)

    def pair(v, k):
        rows = pl.ds(k * BLOCK, BLOCK)
        return v[rows, :load], v[rows, load:]

    def inner(a, b):
        return [fold(a[0] * b[0] + a[1] * b[1]), fold(a[0] * b[1] - a[1] * b[0])]

    def total(parts):
        acc = parts[0]
        for p in parts[1:]:
            acc = [i + j for i, j in zip(acc, p)]
        return [jnp.sum(a, axis=0, keepdims=True) for a in acc]

    moves = exchange(0)
    c_sch.wait()
    prod[...] = jnp.dot(sch[...], qlo[...], preferred_element_type=F32)
    for k in range(nb):
        re, im = image(None, k)
        rows = pl.ds(k * BLOCK, BLOCK)
        u1[rows, :load] = re
        u1[rows, load:] = im
    prod[...] = jnp.dot(sch[...], q[...], preferred_element_type=F32)
    for m in moves:
        m.wait_recv()
    for k in range(nb):
        re, im = image(0, k)
        rows = pl.ds(k * BLOCK, BLOCK)
        v1[rows, :load] = re
        v1[rows, load:] = im
        q[rows, :load] = re.astype(BF16)
        q[rows, load:] = im.astype(BF16)
    moves = exchange(1)
    for k in range(nb):
        rows = pl.ds(k * BLOCK, BLOCK)
        qlo[rows, :] = (v1[rows, :] - q[rows, :].astype(F32)).astype(BF16)
    prod[...] = jnp.dot(sch[...], q[...], preferred_element_type=F32) + jnp.dot(
        sch[...], qlo[...], preferred_element_type=F32
    )
    rows1 = []
    for k in range(nb):
        a = pair(v1, k)
        rows1.append(inner(a, pair(v0, k)) + [fold(abs2(a))])
    rows1 = total(rows1)
    for m in moves:
        m.wait_recv()
    for k in range(nb):
        re, im = image(1, k)
        rows = pl.ds(k * BLOCK, BLOCK)
        v2[rows, :load] = re
        v2[rows, load:] = im
        q[rows, :load] = re.astype(BF16)
        q[rows, load:] = im.astype(BF16)
    moves = exchange(2)
    prod[...] = jnp.dot(sch[...], q[...], preferred_element_type=F32)
    rows2 = []
    for k in range(nb):
        a = pair(v2, k)
        rows2.append(inner(a, pair(v0, k)) + inner(a, pair(v1, k)) + [fold(abs2(a))])
    rows2 = total(rows2)
    for m in moves:
        m.wait_recv()
    rows3 = []
    for k in range(nb):
        a = image(2, k)
        rows3.append(
            inner(a, pair(v0, k)) + inner(a, pair(v1, k)) + inner(a, pair(v2, k)) + [fold(abs2(a))]
        )
    rows3 = total(rows3)

    for i, row in enumerate(rows1 + rows2 + rows3):
        ga_send[i : i + 1, :] = row
    ga_send[15:16, :] = jnp.zeros((1, load), F32)
    moves = [
        send(ga_send, ga_recv.at[i], ga_ss.at[i], ga_rs.at[i], p, f) for i, p in enumerate(group)
    ]
    acc = ga_send[...]
    for i, m in enumerate(moves):
        m.wait_recv()
        acc = acc + ga_recv[i]
    gb_send[...] = acc
    moves = [
        send(gb_send, gb_recv.at[i], gb_ss.at[i], gb_rs.at[i], p, f) for i, p in enumerate(layers)
    ]
    for i, m in enumerate(moves):
        m.wait_recv()
        acc = acc + gb_recv[i]
    row = [acc[i : i + 1, :] for i in range(15)]
    weights = combination((
        (row[0], row[1]), row[2], (row[3], row[4]), (row[5], row[6]), row[7],
        (row[8], row[9]), (row[10], row[11]), (row[12], row[13]), row[14],
    ))
    basis = (v0, v1, u1, v2)

    def solved(start):
        rows = pl.ds(pl.multiple_of(start, CH), CH)
        re = im = None
        for (wr, wi), v in zip(weights, basis):
            a, b = v[rows, :load], v[rows, load:]
            tr, ti = wr * a - wi * b, wr * b + wi * a
            re, im = (tr, ti) if re is None else (re + tr, im + ti)
        return re, im

    def place(half, zt, yt_):
        if half == 0:
            return yt_ * (4 * CH) + (((zt + 1) // 2) % 2) * CH
        return yt_ * (4 * CH) + 2 * CH + (zt // 2) * CH

    z_moves, y_moves = [[], []], [[], []]
    for off in range(NY):
        for h in range(2):
            re, im = solved(place(h, za[h], yt(off)))
            z1s[h, off, :, :load] = re.astype(BF16)
            z1s[h, off, :, load:] = im.astype(BF16)
            z_moves[h].append(
                send(z1s.at[h, off], z1r.at[h, off], z1_ss.at[h, off], z1_rs.at[h, off], s, za[h] * NY + yt(off))
            )
    for off in range(1, NY):
        for h in range(2):
            re, im = solved(place(h, z, yt(off)))
            y1s[h, off - 1, :, :load] = re
            y1s[h, off - 1, :, load:] = im
            y_moves[h].append(
                send(y1s.at[h, off - 1], y1r.at[h, off - 1], y1_ss.at[h, off - 1], y1_rs.at[h, off - 1], s, z * NY + yt(off))
            )
    for h in range(2):
        re, im = solved(place(h, z, y))
        own[h, :, :load] = re
        own[h, :, load:] = im
    c_tbl.wait()

    def sources(h):
        out = [(z * NY + y, own.at[h])]
        out += [(z * NY + yf(off), y1r.at[h, off - 1]) for off in range(1, NY)]
        out += [(za[h] * NY + yf(off), z1r.at[h, off]) for off in range(NY)]
        return out

    def combine(h, zt):
        acc = [None] * NY
        for fs, ref in sources(h):
            re, im = ref[:, :load].astype(F32), ref[:, load:].astype(F32)
            for off in range(NY):
                at = ((zt * NY + yt(off)) * (4 * NY) + fs) * 2
                term = tbl[at] * re + tbl[at + 1] * im
                acc[off] = term if acc[off] is None else acc[off] + term
        return acc

    p_moves = [[], []]
    for h in range(2):
        for m in z_moves[h] + y_moves[h]:
            m.wait_recv()
        for slot, zt in enumerate((za[1 - h], opp)):
            acc = combine(h, zt)
            for off in range(NY):
                p2s[h, slot, off] = acc[off].astype(BF16)
            p_moves[h].append(
                send(p2s.at[h, slot], p2r.at[h, slot], p2_ss.at[h, slot], p2_rs.at[h, slot], s, za[1 - h] * NY + y)
            )
    for h in range(2):
        for slot, zt in ((1, za[h]), (0, z)):
            acc = combine(h, zt)
            for off in range(NY):
                keep[h, slot, off] = acc[off]

    z_moves, y_moves = [[], []], [[], []]
    for h in range(2):
        p_moves[h][1].wait_recv()
        for off in range(NY):
            z3s[h, off] = (keep[h, 1, off] + p2r[h, 1, off].astype(F32)).astype(BF16)
            z_moves[h].append(
                send(z3s.at[h, off], z3r.at[h, off], z3_ss.at[h, off], z3_rs.at[h, off], s, za[h] * NY + yt(off))
            )
    for h in range(2):
        p_moves[h][0].wait_recv()
        for off in range(1, NY):
            y3s[h, off - 1] = keep[h, 0, off] + p2r[h, 0, off].astype(F32)
            y_moves[h].append(
                send(y3s.at[h, off - 1], y3r.at[h, off - 1], y3_ss.at[h, off - 1], y3_rs.at[h, off - 1], s, z * NY + yt(off))
            )
        rows = pl.ds(pl.multiple_of(place(h, z, y), CH), CH)
        out_ref[rows, :] = keep[h, 0, 0] + p2r[h, 0, 0].astype(F32)
    for h in range(2):
        for off in range(1, NY):
            y_moves[h][off - 1].wait_recv()
            rows = pl.ds(pl.multiple_of(place(h, z, yf(off)), CH), CH)
            out_ref[rows, :] = y3r[h, off - 1]
    for h in range(2):
        for off in range(NY):
            z_moves[h][off].wait_recv()
            rows = pl.ds(pl.multiple_of(place(h, za[h], yf(off)), CH), CH)
            out_ref[rows, :] = z3r[h, off].astype(F32)
    for m in sends:
        m.wait_send()


def shards(right_side, schur, match_blocks):
    ni, _, _, loads = right_side.shape
    freqs = lax.axis_size("freq")
    wide = 2 * loads
    dma = pltpu.SemaphoreType.DMA
    vmem = pltpu.VMEM
    out = pl.pallas_call(
        kernel,
        out_shape=jax.ShapeDtypeStruct((ni, loads), F32),
        in_specs=[pl.BlockSpec(memory_space=pltpu.HBM)] * 4,
        out_specs=pl.BlockSpec(memory_space=pltpu.VMEM),
        scratch_shapes=[
            pltpu.SMEM((1, ROUNDS), jnp.int32),
            pltpu.SMEM((2 * freqs * freqs,), F32),
            vmem((2 * ni, loads), F32),
            vmem((2 * ni, ni), BF16),
            vmem((ni, wide), F32),
            vmem((ni, wide), F32),
            vmem((ni, wide), F32),
            vmem((ni, wide), F32),
            vmem((ni, wide), BF16),
            vmem((ni, wide), BF16),
            vmem((2 * ni, wide), F32),
            vmem((3, ROUNDS, BLOCK, wide), BF16),
            vmem((3, ROUNDS, BLOCK, wide), BF16),
            vmem((16, loads), F32),
            vmem((7, 16, loads), F32),
            vmem((16, loads), F32),
            vmem((3, 16, loads), F32),
            vmem((2, NY, CH, wide), BF16),
            vmem((2, NY, CH, wide), BF16),
            vmem((2, NY - 1, CH, wide), F32),
            vmem((2, NY - 1, CH, wide), F32),
            vmem((2, CH, wide), F32),
            vmem((2, 2, NY, CH, loads), BF16),
            vmem((2, 2, NY, CH, loads), BF16),
            vmem((2, 2, NY, CH, loads), F32),
            vmem((2, NY, CH, loads), BF16),
            vmem((2, NY, CH, loads), BF16),
            vmem((2, NY - 1, CH, loads), F32),
            vmem((2, NY - 1, CH, loads), F32),
            dma((4,)),
            dma((3, ROUNDS)), dma((3, ROUNDS)),
            dma((7,)), dma((7,)),
            dma((3,)), dma((3,)),
            dma((2, NY)), dma((2, NY)),
            dma((2, NY - 1)), dma((2, NY - 1)),
            dma((2, 2)), dma((2, 2)),
            dma((2, NY)), dma((2, NY)),
            dma((2, NY - 1)), dma((2, NY - 1)),
        ],
        compiler_params=pltpu.CompilerParams(
            collective_id=0, has_side_effects=True, vmem_limit_bytes=60 * 1024 * 1024
        ),
    )(
        match_blocks,
        jnp.asarray(phase_table(freqs)),
        right_side.reshape(2 * ni, loads),
        schur.reshape(2 * ni, ni),
    )
    return out.reshape(1, ni, loads)


def solution(mesh):
    return jax.shard_map(
        shards,
        mesh=mesh,
        in_specs=(P("sub", "freq", None, None), P("freq", None, "sub", None), P("sub", None)),
        out_specs=P("freq", "sub", None),
        check_vma=False,
    )
```

```python
import jax
import jax.numpy as jnp
import numpy as np
from jax import lax
from jax.experimental import pallas as pl
from jax.experimental.pallas import tpu as pltpu
from jax.sharding import PartitionSpec as P

MESH = pl.DeviceIdType.MESH
F32 = jnp.float32
BF16 = jnp.bfloat16

BLOCK = 128
KAPPA = 0.5
DECAY = 0.5
EPS = 1e-06
ROUNDS = 3
NY = 4
CH = 32
PARTS = 1
PIECE = CH // PARTS


def phase_table(count):
    times = np.arange(count)
    freqs = np.arange(count)
    level = (2 * freqs[None, :] + 1) * times[:, None] % (2 * count)
    angle = np.pi * level / count
    damp = np.exp(DECAY * times / count) / np.sqrt(count)
    table = np.stack([np.cos(angle), -np.sin(angle)], axis=2) * damp[:, None, None]
    return table.astype(np.float32).reshape(-1)


def cmul(a, b):
    return (a[0] * b[0] - a[1] * b[1], a[0] * b[1] + a[1] * b[0])


def conj(a):
    return (a[0], -a[1])


def cadd(a, b):
    return (a[0] + b[0], a[1] + b[1])


def csub(a, b):
    return (a[0] - b[0], a[1] - b[1])


def scale(r, a):
    return (r * a[0], r * a[1])


def abs2(a):
    return a[0] * a[0] + a[1] * a[1]


def divide(a, d):
    return (a[0] / d, a[1] / d)


def combination(g):
    g10, g11, g20, g21, g22, g30, g31, g32, g33 = g
    a0 = divide(g10, g11 + EPS)
    n1 = csub(g10, scale(g11, a0))
    n1 = csub(n1, cmul(conj(a0), g20))
    n1 = cadd(n1, scale(abs2(a0), g21))
    d1 = g11 - 2.0 * cmul(a0, conj(g21))[0] + abs2(a0) * g22
    a1 = divide(n1, jnp.maximum(d1, 0.0) + EPS)
    b = cadd(a0, a1)
    d = cmul(a0, a1)
    n2 = cadd(csub(g10, scale(g11, b)), cmul(d, conj(g21)))
    t = cadd(csub(g20, cmul(b, g21)), scale(g22, d))
    n2 = csub(n2, cmul(conj(b), t))
    t = cadd(csub(g30, cmul(b, g31)), cmul(d, g32))
    n2 = cadd(n2, cmul(conj(d), t))
    d2 = g11 + abs2(b) * g22 + abs2(d) * g33
    d2 = d2 - 2.0 * cmul(b, conj(g21))[0] + 2.0 * cmul(d, conj(g31))[0]
    d2 = d2 - 2.0 * cmul(cmul(conj(b), d), conj(g32))[0]
    a2 = divide(n2, jnp.maximum(d2, 0.0) + EPS)
    w0 = cadd(b, a2)
    w1 = scale(-1.0, cadd(d, cmul(a2, b)))
    wu = scale(-1.0, cmul(a2, a1))
    w2 = cmul(d, a2)
    return w0, w1, wu, w2


def kernel(
    mb_hbm, tbl_hbm, rs_hbm, sch_hbm, out_ref,
    mb, tbl, rs, sch, v0, v1, v2, u1, q, qlo, prod,
    ex_send, ex_recv, ga_send, ga_recv, gb_send, gb_recv,
    z1s, z1r, y1s, y1r, own, p2s, p2r, keep, z3s, z3r, y3s, y3r,
    in_sem, ex_ss, ex_rs, ga_ss, ga_rs, gb_ss, gb_rs,
    z1_ss, z1_rs, y1_ss, y1_rs, p2_ss, p2_rs, z3_ss, z3_rs, y3_ss, y3_rs,
):
    s = lax.axis_index("sub")
    f = lax.axis_index("freq")
    nsub = lax.axis_size("sub")
    z, y = f // NY, f % NY
    ni = v0.shape[0]
    nb = ni // BLOCK
    load = v0.shape[1] // 2

    def flip(bit):
        return s + bit - 2 * bit * ((s // bit) % 2)

    partners = [flip(1), flip(2), flip(8)]
    group = [(s // 8) * 8 + (s + off) % 8 for off in range(1, 8)]
    layers = [(s + 8 * off) % nsub for off in range(1, 4)]
    ze = z + 1 - 2 * (z % 2)
    zo = 3 - z
    opp = 3 - ze
    za = (ze, zo)

    def yt(off):
        return (y + off) % NY

    def yf(off):
        return (y + NY - off) % NY

    sends = []

    def send(src, dst, ss, rsem, sub, freq):
        copy = pltpu.make_async_remote_copy(
            src_ref=src, dst_ref=dst, send_sem=ss, recv_sem=rsem,
            device_id={"sub": sub, "freq": freq}, device_id_type=MESH,
        )
        copy.start()
        sends.append(copy)
        return copy

    c_mb = pltpu.make_async_copy(mb_hbm, mb, in_sem.at[0])
    c_tbl = pltpu.make_async_copy(tbl_hbm, tbl, in_sem.at[1])
    c_sch = pltpu.make_async_copy(sch_hbm, sch, in_sem.at[2])
    c_rs = []
    for k in range(nb):
        rows = pl.ds(2 * BLOCK * k, 2 * BLOCK)
        c_rs.append(pltpu.make_async_copy(rs_hbm.at[rows], rs.at[rows], in_sem.at[3 + k]))
    for copy in c_rs + [c_mb, c_sch, c_tbl]:
        copy.start()

    barrier = pltpu.get_barrier_semaphore()
    peers = [(s, zt * NY + yt(off)) for off in (2, 1, 3, 0) for zt in za]
    peers += [(p, f) for p in layers[::-1] + group]
    peers += [(s, z * NY + yt(off)) for off in range(1, NY)]
    for ps, pf in peers:
        pl.semaphore_signal(barrier, inc=1, device_id={"sub": ps, "freq": pf}, device_id_type=MESH)

    def halves_of(k):
        for c in range(2):
            part = rs[pl.ds(2 * BLOCK * k + c, BLOCK, stride=2), :]
            yield part, pl.ds(k * BLOCK, BLOCK), pl.ds(c * load, load)

    for k in range(nb):
        c_rs[k].wait()
        for part, rows, cols in halves_of(k):
            q[rows, cols] = part.astype(BF16)
    c_mb.wait()
    pl.semaphore_wait(barrier, len(peers))

    def match(r, k):
        gap = (mb[0, r] - k).astype(F32)
        return jnp.maximum(1.0 - gap * gap, 0.0)

    def exchange(j):
        out = []
        for r in (1, 2, 0):
            block = None
            for k in range(nb):
                part = match(r, k) * q[pl.ds(k * BLOCK, BLOCK), :].astype(F32)
                block = part if block is None else block + part
            ex_send[j, r] = block.astype(BF16)
            out.append(send(ex_send.at[j, r], ex_recv.at[j, r], ex_ss.at[j, r], ex_rs.at[j, r], partners[r], f))
        return out

    def image(j, k):
        top = prod[pl.ds(k * BLOCK, BLOCK), :]
        low = prod[pl.ds(ni + k * BLOCK, BLOCK), :]
        re = top[:, :load] - low[:, load:]
        im = top[:, load:] + low[:, :load]
        if j is not None:
            for r in range(ROUNDS):
                weight = KAPPA * match(r, k)
                inc = ex_recv[j, r].astype(F32)
                re = re - weight * inc[:, :load]
                im = im - weight * inc[:, load:]
        return re, im

    def fold(a):
        return jnp.sum(a.reshape(BLOCK // 8, 8, load), axis=0)

    def pair(v, k):
        rows = pl.ds(k * BLOCK, BLOCK)
        return v[rows, :load], v[rows, load:]

    def inner(a, b):
        return [fold(a[0] * b[0] + a[1] * b[1]), fold(a[0] * b[1] - a[1] * b[0])]

    def total(parts):
        acc = parts[0]
        for p in parts[1:]:
            acc = [i + j for i, j in zip(acc, p)]
        return [jnp.sum(a, axis=0, keepdims=True) for a in acc]

    moves = exchange(0)
    for k in range(nb):
        for part, rows, cols in halves_of(k):
            v0[rows, cols] = part
            qlo[rows, cols] = (part - q[rows, cols].astype(F32)).astype(BF16)
    c_sch.wait()
    prod[...] = jnp.dot(sch[...], qlo[...], preferred_element_type=F32)
    for k in range(nb):
        re, im = image(None, k)
        rows = pl.ds(k * BLOCK, BLOCK)
        u1[rows, :load] = re
        u1[rows, load:] = im
    prod[...] = jnp.dot(sch[...], q[...], preferred_element_type=F32)
    for m in moves:
        m.wait_recv()
    for k in range(nb):
        re, im = image(0, k)
        rows = pl.ds(k * BLOCK, BLOCK)
        v1[rows, :load] = re
        v1[rows, load:] = im
        q[rows, :load] = re.astype(BF16)
        q[rows, load:] = im.astype(BF16)
    moves = exchange(1)
    for k in range(nb):
        rows = pl.ds(k * BLOCK, BLOCK)
        qlo[rows, :] = (v1[rows, :] - q[rows, :].astype(F32)).astype(BF16)
    prod[...] = jnp.dot(sch[...], q[...], preferred_element_type=F32) + jnp.dot(
        sch[...], qlo[...], preferred_element_type=F32
    )
    rows1 = []
    for k in range(nb):
        a = pair(v1, k)
        rows1.append(inner(a, pair(v0, k)) + [fold(abs2(a))])
    rows1 = total(rows1)
    for m in moves:
        m.wait_recv()
    for k in range(nb):
        re, im = image(1, k)
        rows = pl.ds(k * BLOCK, BLOCK)
        v2[rows, :load] = re
        v2[rows, load:] = im
        q[rows, :load] = re.astype(BF16)
        q[rows, load:] = im.astype(BF16)
    moves = exchange(2)
    prod[...] = jnp.dot(sch[...], q[...], preferred_element_type=F32)
    rows2 = []
    for k in range(nb):
        a = pair(v2, k)
        rows2.append(inner(a, pair(v0, k)) + inner(a, pair(v1, k)) + [fold(abs2(a))])
    rows2 = total(rows2)
    for m in moves:
        m.wait_recv()
    rows3 = []
    for k in range(nb):
        a = image(2, k)
        rows3.append(
            inner(a, pair(v0, k)) + inner(a, pair(v1, k)) + inner(a, pair(v2, k)) + [fold(abs2(a))]
        )
    rows3 = total(rows3)

    for i, row in enumerate(rows1 + rows2 + rows3):
        ga_send[i : i + 1, :] = row
    ga_send[15:16, :] = jnp.zeros((1, load), F32)
    moves = [
        send(ga_send, ga_recv.at[i], ga_ss.at[i], ga_rs.at[i], p, f) for i, p in enumerate(group)
    ]
    acc = ga_send[...]
    for i, m in enumerate(moves):
        m.wait_recv()
        acc = acc + ga_recv[i]
    gb_send[...] = acc
    moves = [
        send(gb_send, gb_recv.at[i], gb_ss.at[i], gb_rs.at[i], p, f) for i, p in enumerate(layers)
    ]
    for i, m in enumerate(moves):
        m.wait_recv()
        acc = acc + gb_recv[i]
    row = [acc[i : i + 1, :] for i in range(15)]
    weights = combination((
        (row[0], row[1]), row[2], (row[3], row[4]), (row[5], row[6]), row[7],
        (row[8], row[9]), (row[10], row[11]), (row[12], row[13]), row[14],
    ))
    basis = (v0, v1, u1, v2)

    def solved(start):
        rows = pl.ds(pl.multiple_of(start, PIECE), PIECE)
        re = im = None
        for (wr, wi), v in zip(weights, basis):
            a, b = v[rows, :load], v[rows, load:]
            tr, ti = wr * a - wi * b, wr * b + wi * a
            re, im = (tr, ti) if re is None else (re + tr, im + ti)
        return re, im

    def place(c, half, zt, yt_):
        first = yt_ * (4 * CH) + c * PIECE
        if half == 0:
            return first + (((zt + 1) // 2) % 2) * CH
        return first + 2 * CH + (zt // 2) * CH

    parts, halves, offs = range(PARTS), range(2), range(NY)

    z_moves, y_moves = {}, {}
    for c in parts:
        for off in (2, 1, 3, 0):
            for h in halves:
                re, im = solved(place(c, h, za[h], yt(off)))
                z1s[c, h, off, :, :load] = re.astype(BF16)
                z1s[c, h, off, :, load:] = im.astype(BF16)
                z_moves[c, h, off] = send(
                    z1s.at[c, h, off], z1r.at[c, h, off], z1_ss.at[c, h, off], z1_rs.at[c, h, off],
                    s, za[h] * NY + yt(off),
                )
        for off in (2, 1, 3):
            for h in halves:
                re, im = solved(place(c, h, z, yt(off)))
                y1s[c, h, off - 1, :, :load] = re
                y1s[c, h, off - 1, :, load:] = im
                y_moves[c, h, off] = send(
                    y1s.at[c, h, off - 1], y1r.at[c, h, off - 1], y1_ss.at[c, h, off - 1], y1_rs.at[c, h, off - 1],
                    s, z * NY + yt(off),
                )
    for c in parts:
        for h in halves:
            re, im = solved(place(c, h, z, y))
            own[c, h, :, :load] = re
            own[c, h, :, load:] = im
    c_tbl.wait()

    def sources(c, h):
        out = [(z * NY + y, own.at[c, h])]
        out += [(z * NY + yf(off), y1r.at[c, h, off - 1]) for off in offs[1:]]
        out += [(za[h] * NY + yf(off), z1r.at[c, h, off]) for off in offs]
        return out

    def combine(c, h, zt):
        acc = [None] * NY
        for fs, ref in sources(c, h):
            re, im = ref[:, :load].astype(F32), ref[:, load:].astype(F32)
            for off in offs:
                at = ((zt * NY + yt(off)) * (4 * NY) + fs) * 2
                term = tbl[at] * re + tbl[at + 1] * im
                acc[off] = term if acc[off] is None else acc[off] + term
        return acc

    p_moves = {}
    for c in parts:
        for h in halves:
            for off in offs[1:]:
                y_moves[c, h, off].wait_recv()
            for off in offs:
                z_moves[c, h, off].wait_recv()
            for slot, zt in ((1, opp), (0, za[1 - h])):
                acc = combine(c, h, zt)
                for off in offs:
                    p2s[c, h, slot, off] = acc[off].astype(BF16)
                p_moves[c, h, slot] = send(
                    p2s.at[c, h, slot], p2r.at[c, h, slot], p2_ss.at[c, h, slot], p2_rs.at[c, h, slot],
                    s, za[1 - h] * NY + y,
                )
        for h in halves:
            for slot, zt in ((1, za[h]), (0, z)):
                acc = combine(c, h, zt)
                for off in offs:
                    keep[c, h, slot, off] = acc[off]

    z_moves, y_moves = {}, {}
    for c in parts:
        for h in halves:
            p_moves[c, h, 1].wait_recv()
            for off in (2, 1, 3, 0):
                z3s[c, h, off] = (keep[c, h, 1, off] + p2r[c, h, 1, off].astype(F32)).astype(BF16)
                z_moves[c, h, off] = send(
                    z3s.at[c, h, off], z3r.at[c, h, off], z3_ss.at[c, h, off], z3_rs.at[c, h, off],
                    s, za[h] * NY + yt(off),
                )
        for h in halves:
            p_moves[c, h, 0].wait_recv()
            for off in (2, 1, 3):
                y3s[c, h, off - 1] = keep[c, h, 0, off] + p2r[c, h, 0, off].astype(F32)
                y_moves[c, h, off] = send(
                    y3s.at[c, h, off - 1], y3r.at[c, h, off - 1], y3_ss.at[c, h, off - 1], y3_rs.at[c, h, off - 1],
                    s, z * NY + yt(off),
                )
            rows = pl.ds(pl.multiple_of(place(c, h, z, y), PIECE), PIECE)
            out_ref[rows, :] = keep[c, h, 0, 0] + p2r[c, h, 0, 0].astype(F32)
    for c in parts:
        for h in halves:
            for off in offs[1:]:
                y_moves[c, h, off].wait_recv()
                rows = pl.ds(pl.multiple_of(place(c, h, z, yf(off)), PIECE), PIECE)
                out_ref[rows, :] = y3r[c, h, off - 1]
        for h in halves:
            for off in offs:
                z_moves[c, h, off].wait_recv()
                rows = pl.ds(pl.multiple_of(place(c, h, za[h], yf(off)), PIECE), PIECE)
                out_ref[rows, :] = z3r[c, h, off].astype(F32)
    for m in sends:
        m.wait_send()


def shards(right_side, schur, match_blocks):
    ni, _, _, loads = right_side.shape
    freqs = lax.axis_size("freq")
    wide = 2 * loads
    dma = pltpu.SemaphoreType.DMA
    vmem = pltpu.VMEM
    out = pl.pallas_call(
        kernel,
        out_shape=pltpu.VMEM((ni, loads), F32),
        in_specs=[pl.BlockSpec(memory_space=pltpu.HBM)] * 4,
        out_specs=pl.BlockSpec(memory_space=pltpu.VMEM),
        scratch_shapes=[
            pltpu.SMEM((1, ROUNDS), jnp.int32),
            pltpu.SMEM((2 * freqs * freqs,), F32),
            vmem((2 * ni, loads), F32),
            vmem((2 * ni, ni), BF16),
            vmem((ni, wide), F32),
            vmem((ni, wide), F32),
            vmem((ni, wide), F32),
            vmem((ni, wide), F32),
            vmem((ni, wide), BF16),
            vmem((ni, wide), BF16),
            vmem((2 * ni, wide), F32),
            vmem((3, ROUNDS, BLOCK, wide), BF16),
            vmem((3, ROUNDS, BLOCK, wide), BF16),
            vmem((16, loads), F32),
            vmem((7, 16, loads), F32),
            vmem((16, loads), F32),
            vmem((3, 16, loads), F32),
            vmem((PARTS, 2, NY, PIECE, wide), BF16),
            vmem((PARTS, 2, NY, PIECE, wide), BF16),
            vmem((PARTS, 2, NY - 1, PIECE, wide), F32),
            vmem((PARTS, 2, NY - 1, PIECE, wide), F32),
            vmem((PARTS, 2, PIECE, wide), F32),
            vmem((PARTS, 2, 2, NY, PIECE, loads), BF16),
            vmem((PARTS, 2, 2, NY, PIECE, loads), BF16),
            vmem((PARTS, 2, 2, NY, PIECE, loads), F32),
            vmem((PARTS, 2, NY, PIECE, loads), BF16),
            vmem((PARTS, 2, NY, PIECE, loads), BF16),
            vmem((PARTS, 2, NY - 1, PIECE, loads), F32),
            vmem((PARTS, 2, NY - 1, PIECE, loads), F32),
            dma((3 + ni // BLOCK,)),
            dma((3, ROUNDS)), dma((3, ROUNDS)),
            dma((7,)), dma((7,)),
            dma((3,)), dma((3,)),
            dma((PARTS, 2, NY)), dma((PARTS, 2, NY)),
            dma((PARTS, 2, NY - 1)), dma((PARTS, 2, NY - 1)),
            dma((PARTS, 2, 2)), dma((PARTS, 2, 2)),
            dma((PARTS, 2, NY)), dma((PARTS, 2, NY)),
            dma((PARTS, 2, NY - 1)), dma((PARTS, 2, NY - 1)),
        ],
        compiler_params=pltpu.CompilerParams(
            collective_id=0, has_side_effects=True, vmem_limit_bytes=60 * 1024 * 1024
        ),
    )(
        match_blocks,
        jnp.asarray(phase_table(freqs)),
        right_side.reshape(2 * ni, loads),
        schur.reshape(2 * ni, ni),
    )
    return out.reshape(1, ni, loads)


def solution(mesh):
    return jax.shard_map(
        shards,
        mesh=mesh,
        in_specs=(P("sub", "freq", None, None), P("freq", None, "sub", None), P("sub", None)),
        out_specs=P("freq", "sub", None),
        check_vma=False,
    )
```

```python
import jax
import jax.numpy as jnp
import numpy as np
from jax import lax
from jax.experimental import pallas as pl
from jax.experimental.pallas import tpu as pltpu
from jax.sharding import PartitionSpec as P

MESH = pl.DeviceIdType.MESH
F32 = jnp.float32
BF16 = jnp.bfloat16

BLOCK = 128
KAPPA = 0.5
DECAY = 0.5
EPS = 1e-06
ROUNDS = 3
NY = 4
CH = 32
PARTS = 2
PIECE = CH // PARTS


def phase_table(count):
    times = np.arange(count)
    freqs = np.arange(count)
    level = (2 * freqs[None, :] + 1) * times[:, None] % (2 * count)
    angle = np.pi * level / count
    damp = np.exp(DECAY * times / count) / np.sqrt(count)
    table = np.stack([np.cos(angle), -np.sin(angle)], axis=2) * damp[:, None, None]
    return table.astype(np.float32).reshape(-1)


def cmul(a, b):
    return (a[0] * b[0] - a[1] * b[1], a[0] * b[1] + a[1] * b[0])


def conj(a):
    return (a[0], -a[1])


def cadd(a, b):
    return (a[0] + b[0], a[1] + b[1])


def csub(a, b):
    return (a[0] - b[0], a[1] - b[1])


def scale(r, a):
    return (r * a[0], r * a[1])


def abs2(a):
    return a[0] * a[0] + a[1] * a[1]


def divide(a, d):
    return (a[0] / d, a[1] / d)


def combination(g):
    g10, g11, g20, g21, g22, g30, g31, g32, g33 = g
    a0 = divide(g10, g11 + EPS)
    n1 = csub(g10, scale(g11, a0))
    n1 = csub(n1, cmul(conj(a0), g20))
    n1 = cadd(n1, scale(abs2(a0), g21))
    d1 = g11 - 2.0 * cmul(a0, conj(g21))[0] + abs2(a0) * g22
    a1 = divide(n1, jnp.maximum(d1, 0.0) + EPS)
    b = cadd(a0, a1)
    d = cmul(a0, a1)
    n2 = cadd(csub(g10, scale(g11, b)), cmul(d, conj(g21)))
    t = cadd(csub(g20, cmul(b, g21)), scale(g22, d))
    n2 = csub(n2, cmul(conj(b), t))
    t = cadd(csub(g30, cmul(b, g31)), cmul(d, g32))
    n2 = cadd(n2, cmul(conj(d), t))
    d2 = g11 + abs2(b) * g22 + abs2(d) * g33
    d2 = d2 - 2.0 * cmul(b, conj(g21))[0] + 2.0 * cmul(d, conj(g31))[0]
    d2 = d2 - 2.0 * cmul(cmul(conj(b), d), conj(g32))[0]
    a2 = divide(n2, jnp.maximum(d2, 0.0) + EPS)
    w0 = cadd(b, a2)
    w1 = scale(-1.0, cadd(d, cmul(a2, b)))
    wu = scale(-1.0, cmul(a2, a1))
    w2 = cmul(d, a2)
    return w0, w1, wu, w2


def kernel(
    mb_hbm, tbl_hbm, rs_hbm, sch_hbm, out_ref,
    mb, tbl, rs, sch, v0, v1, v2, u1, q, qlo, prod,
    ex_send, ex_recv, ga_send, ga_recv, gb_send, gb_recv,
    z1s, z1r, y1s, y1r, own, p2s, p2r, keep, z3s, z3r, y3s, y3r,
    in_sem, ex_ss, ex_rs, ga_ss, ga_rs, gb_ss, gb_rs,
    z1_ss, z1_rs, y1_ss, y1_rs, p2_ss, p2_rs, z3_ss, z3_rs, y3_ss, y3_rs,
):
    s = lax.axis_index("sub")
    f = lax.axis_index("freq")
    nsub = lax.axis_size("sub")
    z, y = f // NY, f % NY
    ni = v0.shape[0]
    nb = ni // BLOCK
    load = v0.shape[1] // 2

    def flip(bit):
        return s + bit - 2 * bit * ((s // bit) % 2)

    partners = [flip(1), flip(2), flip(8)]
    group = [(s // 8) * 8 + (s + off) % 8 for off in (7, 6, 5, 4, 3, 2, 1)]
    layers = [(s + 8 * off) % nsub for off in range(1, 4)]
    ze = z + 1 - 2 * (z % 2)
    zo = 3 - z
    opp = 3 - ze
    za = (ze, zo)

    def yt(off):
        return (y + off) % NY

    def yf(off):
        return (y + NY - off) % NY

    sends = []

    def left(copies):
        for m in copies:
            m.wait_send()
        sends[:] = [m for m in sends if all(m is not o for o in copies)]


    def send(src, dst, ss, rsem, sub, freq):
        copy = pltpu.make_async_remote_copy(
            src_ref=src, dst_ref=dst, send_sem=ss, recv_sem=rsem,
            device_id={"sub": sub, "freq": freq}, device_id_type=MESH,
        )
        copy.start()
        sends.append(copy)
        return copy

    c_mb = pltpu.make_async_copy(mb_hbm, mb, in_sem.at[0])
    c_tbl = pltpu.make_async_copy(tbl_hbm, tbl, in_sem.at[1])
    c_sch = pltpu.make_async_copy(sch_hbm, sch, in_sem.at[2])
    c_rs = []
    for k in range(nb):
        rows = pl.ds(2 * BLOCK * k, 2 * BLOCK)
        c_rs.append(pltpu.make_async_copy(rs_hbm.at[rows], rs.at[rows], in_sem.at[3 + k]))
    for copy in c_rs + [c_mb, c_sch, c_tbl]:
        copy.start()

    barrier = pltpu.get_barrier_semaphore()
    peers = [(s, zt * NY + yt(off)) for off in (2, 1, 3, 0) for zt in za]
    peers += [(p, f) for p in layers[::-1] + group]
    peers += [(s, z * NY + yt(off)) for off in range(1, NY)]
    for ps, pf in peers:
        pl.semaphore_signal(barrier, inc=1, device_id={"sub": ps, "freq": pf}, device_id_type=MESH)

    def halves_of(k):
        for c in range(2):
            part = rs[pl.ds(2 * BLOCK * k + c, BLOCK, stride=2), :]
            yield part, pl.ds(k * BLOCK, BLOCK), pl.ds(c * load, load)

    for k in range(nb):
        c_rs[k].wait()
        for part, rows, cols in halves_of(k):
            q[rows, cols] = part.astype(BF16)
    c_mb.wait()
    pl.semaphore_wait(barrier, len(peers))

    def match(r, k):
        gap = (mb[0, r] - k).astype(F32)
        return jnp.maximum(1.0 - gap * gap, 0.0)

    def exchange(j):
        out = []
        for r in (1, 2, 0):
            block = None
            for k in range(nb):
                part = match(r, k) * q[pl.ds(k * BLOCK, BLOCK), :].astype(F32)
                block = part if block is None else block + part
            ex_send[j, r] = block.astype(BF16)
            out.append(send(ex_send.at[j, r], ex_recv.at[j, r], ex_ss.at[j, r], ex_rs.at[j, r], partners[r], f))
        return out

    def image(j, k):
        top = prod[pl.ds(k * BLOCK, BLOCK), :]
        low = prod[pl.ds(ni + k * BLOCK, BLOCK), :]
        re = top[:, :load] - low[:, load:]
        im = top[:, load:] + low[:, :load]
        if j is not None:
            for r in range(ROUNDS):
                weight = KAPPA * match(r, k)
                inc = ex_recv[j, r].astype(F32)
                re = re - weight * inc[:, :load]
                im = im - weight * inc[:, load:]
        return re, im

    def fold(a):
        return jnp.sum(a.reshape(BLOCK // 8, 8, load), axis=0)

    def pair(v, k):
        rows = pl.ds(k * BLOCK, BLOCK)
        return v[rows, :load], v[rows, load:]

    def inner(a, b):
        return [fold(a[0] * b[0] + a[1] * b[1]), fold(a[0] * b[1] - a[1] * b[0])]

    def total(parts):
        acc = parts[0]
        for p in parts[1:]:
            acc = [i + j for i, j in zip(acc, p)]
        return [jnp.sum(a, axis=0, keepdims=True) for a in acc]

    moves = exchange(0)
    for k in range(nb):
        for part, rows, cols in halves_of(k):
            v0[rows, cols] = part
            qlo[rows, cols] = (part - q[rows, cols].astype(F32)).astype(BF16)
    c_sch.wait()
    prod[...] = jnp.dot(sch[...], qlo[...], preferred_element_type=F32)
    for k in range(nb):
        re, im = image(None, k)
        rows = pl.ds(k * BLOCK, BLOCK)
        u1[rows, :load] = re
        u1[rows, load:] = im
    prod[...] = jnp.dot(sch[...], q[...], preferred_element_type=F32)
    for m in moves:
        m.wait_recv()
    for k in range(nb):
        re, im = image(0, k)
        rows = pl.ds(k * BLOCK, BLOCK)
        v1[rows, :load] = re
        v1[rows, load:] = im
        q[rows, :load] = re.astype(BF16)
        q[rows, load:] = im.astype(BF16)
    moves = exchange(1)
    for k in range(nb):
        rows = pl.ds(k * BLOCK, BLOCK)
        qlo[rows, :] = (v1[rows, :] - q[rows, :].astype(F32)).astype(BF16)
    prod[...] = jnp.dot(sch[...], q[...], preferred_element_type=F32) + jnp.dot(
        sch[...], qlo[...], preferred_element_type=F32
    )
    rows1 = []
    for k in range(nb):
        a = pair(v1, k)
        rows1.append(inner(a, pair(v0, k)) + [fold(abs2(a))])
    rows1 = total(rows1)
    for m in moves:
        m.wait_recv()
    for k in range(nb):
        re, im = image(1, k)
        rows = pl.ds(k * BLOCK, BLOCK)
        v2[rows, :load] = re
        v2[rows, load:] = im
        q[rows, :load] = re.astype(BF16)
        q[rows, load:] = im.astype(BF16)
    moves = exchange(2)
    prod[...] = jnp.dot(sch[...], q[...], preferred_element_type=F32)
    rows2 = []
    for k in range(nb):
        a = pair(v2, k)
        rows2.append(inner(a, pair(v0, k)) + inner(a, pair(v1, k)) + [fold(abs2(a))])
    rows2 = total(rows2)
    for m in moves:
        m.wait_recv()
    rows3 = []
    for k in range(nb):
        a = image(2, k)
        rows3.append(
            inner(a, pair(v0, k)) + inner(a, pair(v1, k)) + inner(a, pair(v2, k)) + [fold(abs2(a))]
        )
    rows3 = total(rows3)

    for i, row in enumerate(rows1 + rows2 + rows3):
        ga_send[i : i + 1, :] = row
    ga_send[15:16, :] = jnp.zeros((1, load), F32)
    moves = [
        send(ga_send, ga_recv.at[i], ga_ss.at[i], ga_rs.at[i], p, f) for i, p in enumerate(group)
    ]
    acc = ga_send[...]
    for i, m in enumerate(moves):
        m.wait_recv()
        acc = acc + ga_recv[i]
    gb_send[...] = acc
    moves = [
        send(gb_send, gb_recv.at[i], gb_ss.at[i], gb_rs.at[i], p, f) for i, p in enumerate(layers)
    ]
    for i, m in enumerate(moves):
        m.wait_recv()
        acc = acc + gb_recv[i]
    row = [acc[i : i + 1, :] for i in range(15)]
    weights = combination((
        (row[0], row[1]), row[2], (row[3], row[4]), (row[5], row[6]), row[7],
        (row[8], row[9]), (row[10], row[11]), (row[12], row[13]), row[14],
    ))
    basis = (v0, v1, u1, v2)

    def solved(start):
        rows = pl.ds(pl.multiple_of(start, PIECE), PIECE)
        re = im = None
        for (wr, wi), v in zip(weights, basis):
            a, b = v[rows, :load], v[rows, load:]
            tr, ti = wr * a - wi * b, wr * b + wi * a
            re, im = (tr, ti) if re is None else (re + tr, im + ti)
        return re, im

    def place(c, half, zt, yt_):
        first = yt_ * (4 * CH) + c * PIECE
        if half == 0:
            return first + (((zt + 1) // 2) % 2) * CH
        return first + 2 * CH + (zt // 2) * CH

    parts, halves, offs = range(PARTS), range(2), range(NY)

    z_moves, y_moves = {}, {}
    for c in parts:
        if c:
            left([z_moves[c - 1, h, off] for h in halves for off in offs])
        for off in (2, 1, 3, 0):
            for h in halves:
                re, im = solved(place(c, h, za[h], yt(off)))
                z1s[c, h, off, :, :load] = re.astype(BF16)
                z1s[c, h, off, :, load:] = im.astype(BF16)
                z_moves[c, h, off] = send(
                    z1s.at[c, h, off], z1r.at[c, h, off], z1_ss.at[c, h, off], z1_rs.at[c, h, off],
                    s, za[h] * NY + yt(off),
                )
        for off in (2, 1, 3):
            for h in halves:
                re, im = solved(place(c, h, z, yt(off)))
                y1s[c, h, off - 1, :, :load] = re
                y1s[c, h, off - 1, :, load:] = im
                y_moves[c, h, off] = send(
                    y1s.at[c, h, off - 1], y1r.at[c, h, off - 1], y1_ss.at[c, h, off - 1], y1_rs.at[c, h, off - 1],
                    s, z * NY + yt(off),
                )
    for c in parts:
        for h in halves:
            re, im = solved(place(c, h, z, y))
            own[c, h, :, :load] = re
            own[c, h, :, load:] = im
    c_tbl.wait()

    def sources(c, h):
        out = [(z * NY + y, own.at[c, h])]
        out += [(z * NY + yf(off), y1r.at[c, h, off - 1]) for off in offs[1:]]
        out += [(za[h] * NY + yf(off), z1r.at[c, h, off]) for off in offs]
        return out

    def combine(c, h, zt):
        acc = [None] * NY
        for fs, ref in sources(c, h):
            re, im = ref[:, :load].astype(F32), ref[:, load:].astype(F32)
            for off in offs:
                at = ((zt * NY + yt(off)) * (4 * NY) + fs) * 2
                term = tbl[at] * re + tbl[at + 1] * im
                acc[off] = term if acc[off] is None else acc[off] + term
        return acc

    p_moves = {}

    def pass_on(c, h, slot):
        acc = combine(c, h, opp if slot else za[1 - h])
        for off in offs:
            p2s[c, h, slot, off] = acc[off].astype(BF16)
        p_moves[c, h, slot] = send(
            p2s.at[c, h, slot], p2r.at[c, h, slot], p2_ss.at[c, h, slot], p2_rs.at[c, h, slot],
            s, za[1 - h] * NY + y,
        )

    def hold(c, h, slot):
        acc = combine(c, h, za[h] if slot else z)
        for off in offs:
            keep[c, h, slot, off] = acc[off]

    for c in parts:
        for h in halves:
            for off in offs[1:]:
                y_moves[c, h, off].wait_recv()
            for off in offs:
                z_moves[c, h, off].wait_recv()
            pass_on(c, h, 1)
    left([p_moves[c, h, 1] for c in parts for h in halves])
    for c in parts:
        for h in halves:
            pass_on(c, h, 0)
    for slot in (1, 0):
        for c in parts:
            for h in halves:
                hold(c, h, slot)

    z_moves, y_moves = {}, {}
    for c in parts:
        for h in halves:
            p_moves[c, h, 1].wait_recv()
            for off in (2, 1, 3, 0):
                z3s[c, h, off] = (keep[c, h, 1, off] + p2r[c, h, 1, off].astype(F32)).astype(BF16)
                z_moves[c, h, off] = send(
                    z3s.at[c, h, off], z3r.at[c, h, off], z3_ss.at[c, h, off], z3_rs.at[c, h, off],
                    s, za[h] * NY + yt(off),
                )
    for c in parts:
        for h in halves:
            p_moves[c, h, 0].wait_recv()
            for off in (2, 1, 3):
                y3s[c, h, off - 1] = keep[c, h, 0, off] + p2r[c, h, 0, off].astype(F32)
                y_moves[c, h, off] = send(
                    y3s.at[c, h, off - 1], y3r.at[c, h, off - 1], y3_ss.at[c, h, off - 1], y3_rs.at[c, h, off - 1],
                    s, z * NY + yt(off),
                )
            rows = pl.ds(pl.multiple_of(place(c, h, z, y), PIECE), PIECE)
            out_ref[rows, :] = keep[c, h, 0, 0] + p2r[c, h, 0, 0].astype(F32)
    for c in parts:
        for h in halves:
            for off in offs[1:]:
                y_moves[c, h, off].wait_recv()
                rows = pl.ds(pl.multiple_of(place(c, h, z, yf(off)), PIECE), PIECE)
                out_ref[rows, :] = y3r[c, h, off - 1]
        for h in halves:
            for off in offs:
                z_moves[c, h, off].wait_recv()
                rows = pl.ds(pl.multiple_of(place(c, h, za[h], yf(off)), PIECE), PIECE)
                out_ref[rows, :] = z3r[c, h, off].astype(F32)
    for m in sends:
        m.wait_send()


def shards(right_side, schur, match_blocks):
    ni, _, _, loads = right_side.shape
    freqs = lax.axis_size("freq")
    wide = 2 * loads
    dma = pltpu.SemaphoreType.DMA
    vmem = pltpu.VMEM
    out = pl.pallas_call(
        kernel,
        out_shape=pltpu.VMEM((ni, loads), F32),
        in_specs=[pl.BlockSpec(memory_space=pltpu.HBM)] * 4,
        out_specs=pl.BlockSpec(memory_space=pltpu.VMEM),
        scratch_shapes=[
            pltpu.SMEM((1, ROUNDS), jnp.int32),
            pltpu.SMEM((2 * freqs * freqs,), F32),
            vmem((2 * ni, loads), F32),
            vmem((2 * ni, ni), BF16),
            vmem((ni, wide), F32),
            vmem((ni, wide), F32),
            vmem((ni, wide), F32),
            vmem((ni, wide), F32),
            vmem((ni, wide), BF16),
            vmem((ni, wide), BF16),
            vmem((2 * ni, wide), F32),
            vmem((3, ROUNDS, BLOCK, wide), BF16),
            vmem((3, ROUNDS, BLOCK, wide), BF16),
            vmem((16, loads), F32),
            vmem((7, 16, loads), F32),
            vmem((16, loads), F32),
            vmem((3, 16, loads), F32),
            vmem((PARTS, 2, NY, PIECE, wide), BF16),
            vmem((PARTS, 2, NY, PIECE, wide), BF16),
            vmem((PARTS, 2, NY - 1, PIECE, wide), F32),
            vmem((PARTS, 2, NY - 1, PIECE, wide), F32),
            vmem((PARTS, 2, PIECE, wide), F32),
            vmem((PARTS, 2, 2, NY, PIECE, loads), BF16),
            vmem((PARTS, 2, 2, NY, PIECE, loads), BF16),
            vmem((PARTS, 2, 2, NY, PIECE, loads), F32),
            vmem((PARTS, 2, NY, PIECE, loads), BF16),
            vmem((PARTS, 2, NY, PIECE, loads), BF16),
            vmem((PARTS, 2, NY - 1, PIECE, loads), F32),
            vmem((PARTS, 2, NY - 1, PIECE, loads), F32),
            dma((3 + ni // BLOCK,)),
            dma((3, ROUNDS)), dma((3, ROUNDS)),
            dma((7,)), dma((7,)),
            dma((3,)), dma((3,)),
            dma((PARTS, 2, NY)), dma((PARTS, 2, NY)),
            dma((PARTS, 2, NY - 1)), dma((PARTS, 2, NY - 1)),
            dma((PARTS, 2, 2)), dma((PARTS, 2, 2)),
            dma((PARTS, 2, NY)), dma((PARTS, 2, NY)),
            dma((PARTS, 2, NY - 1)), dma((PARTS, 2, NY - 1)),
        ],
        compiler_params=pltpu.CompilerParams(
            collective_id=0, has_side_effects=True, vmem_limit_bytes=60 * 1024 * 1024
        ),
    )(
        match_blocks,
        jnp.asarray(phase_table(freqs)),
        right_side.reshape(2 * ni, loads),
        schur.reshape(2 * ni, ni),
    )
    return out.reshape(1, ni, loads)


def solution(mesh):
    return jax.shard_map(
        shards,
        mesh=mesh,
        in_specs=(P("sub", "freq", None, None), P("freq", None, "sub", None), P("sub", None)),
        out_specs=P("freq", "sub", None),
        check_vma=False,
    )
```

```python
import jax
import jax.numpy as jnp
import numpy as np
from jax import lax
from jax.experimental import pallas as pl
from jax.experimental.pallas import tpu as pltpu
from jax.sharding import PartitionSpec as P

MESH = pl.DeviceIdType.MESH
F32 = jnp.float32
BF16 = jnp.bfloat16

BLOCK = 128
KAPPA = 0.5
DECAY = 0.5
EPS = 1e-06
ROUNDS = 3
NY = 4
CH = 32
PARTS = 2
PIECE = CH // PARTS


def phase_table(count):
    times = np.arange(count)
    freqs = np.arange(count)
    level = (2 * freqs[None, :] + 1) * times[:, None] % (2 * count)
    angle = np.pi * level / count
    damp = np.exp(DECAY * times / count) / np.sqrt(count)
    table = np.stack([np.cos(angle), -np.sin(angle)], axis=2) * damp[:, None, None]
    return table.astype(np.float32).reshape(-1)


def cmul(a, b):
    return (a[0] * b[0] - a[1] * b[1], a[0] * b[1] + a[1] * b[0])


def conj(a):
    return (a[0], -a[1])


def cadd(a, b):
    return (a[0] + b[0], a[1] + b[1])


def csub(a, b):
    return (a[0] - b[0], a[1] - b[1])


def scale(r, a):
    return (r * a[0], r * a[1])


def abs2(a):
    return a[0] * a[0] + a[1] * a[1]


def divide(a, d):
    return (a[0] / d, a[1] / d)


def combination(g):
    g10, g11, g20, g21, g22, g30, g31, g32, g33 = g
    a0 = divide(g10, g11 + EPS)
    n1 = csub(g10, scale(g11, a0))
    n1 = csub(n1, cmul(conj(a0), g20))
    n1 = cadd(n1, scale(abs2(a0), g21))
    d1 = g11 - 2.0 * cmul(a0, conj(g21))[0] + abs2(a0) * g22
    a1 = divide(n1, jnp.maximum(d1, 0.0) + EPS)
    b = cadd(a0, a1)
    d = cmul(a0, a1)
    n2 = cadd(csub(g10, scale(g11, b)), cmul(d, conj(g21)))
    t = cadd(csub(g20, cmul(b, g21)), scale(g22, d))
    n2 = csub(n2, cmul(conj(b), t))
    t = cadd(csub(g30, cmul(b, g31)), cmul(d, g32))
    n2 = cadd(n2, cmul(conj(d), t))
    d2 = g11 + abs2(b) * g22 + abs2(d) * g33
    d2 = d2 - 2.0 * cmul(b, conj(g21))[0] + 2.0 * cmul(d, conj(g31))[0]
    d2 = d2 - 2.0 * cmul(cmul(conj(b), d), conj(g32))[0]
    a2 = divide(n2, jnp.maximum(d2, 0.0) + EPS)
    w0 = cadd(b, a2)
    w1 = scale(-1.0, cadd(d, cmul(a2, b)))
    wu = scale(-1.0, cmul(a2, a1))
    w2 = cmul(d, a2)
    return w0, w1, wu, w2


def kernel(
    mb_hbm, tbl_hbm, rs_hbm, sch_hbm, out_ref,
    mb, tbl, rs, sch, v0, v1, v2, u1, q, qlo, prod,
    ex_send, ex_recv, ga_send, ga_recv, gb_send, gb_recv,
    z1s, z1r, y1s, y1r, own, p2s, p2r, keep, z3s, z3r, y3s, y3r,
    in_sem, ex_ss, ex_rs, ga_ss, ga_rs, gb_ss, gb_rs,
    z1_ss, z1_rs, y1_ss, y1_rs, p2_ss, p2_rs, z3_ss, z3_rs, y3_ss, y3_rs,
):
    s = lax.axis_index("sub")
    f = lax.axis_index("freq")
    nsub = lax.axis_size("sub")
    z, y = f // NY, f % NY
    ni = v0.shape[0]
    nb = ni // BLOCK
    load = v0.shape[1] // 2

    def flip(bit):
        return s + bit - 2 * bit * ((s // bit) % 2)

    partners = [flip(1), flip(2), flip(8)]
    group = [(s // 8) * 8 + (s + off) % 8 for off in (7, 6, 5, 4, 3, 2, 1)]
    layers = [(s + 8 * off) % nsub for off in range(1, 4)]
    ze = z + 1 - 2 * (z % 2)
    zo = 3 - z
    opp = 3 - ze
    za = (ze, zo)

    def yt(off):
        return (y + off) % NY

    def yf(off):
        return (y + NY - off) % NY

    sends = []

    def left(copies):
        for m in copies:
            m.wait_send()
        sends[:] = [m for m in sends if all(m is not o for o in copies)]


    def send(src, dst, ss, rsem, sub, freq):
        copy = pltpu.make_async_remote_copy(
            src_ref=src, dst_ref=dst, send_sem=ss, recv_sem=rsem,
            device_id={"sub": sub, "freq": freq}, device_id_type=MESH,
        )
        copy.start()
        sends.append(copy)
        return copy

    c_mb = pltpu.make_async_copy(mb_hbm, mb, in_sem.at[0])
    c_tbl = pltpu.make_async_copy(tbl_hbm, tbl, in_sem.at[1])
    c_sch = pltpu.make_async_copy(sch_hbm, sch, in_sem.at[2])
    c_rs = []
    for k in range(nb):
        rows = pl.ds(2 * BLOCK * k, 2 * BLOCK)
        c_rs.append(pltpu.make_async_copy(rs_hbm.at[rows], rs.at[rows], in_sem.at[3 + k]))
    for copy in c_rs + [c_mb, c_sch, c_tbl]:
        copy.start()

    barrier = pltpu.get_barrier_semaphore()
    peers = [(s, zt * NY + yt(off)) for off in (2, 1, 3, 0) for zt in za]
    peers += [(p, f) for p in layers[::-1] + group]
    peers += [(s, z * NY + yt(off)) for off in range(1, NY)]
    for ps, pf in peers:
        pl.semaphore_signal(barrier, inc=1, device_id={"sub": ps, "freq": pf}, device_id_type=MESH)

    def halves_of(k):
        for c in range(2):
            part = rs[pl.ds(2 * BLOCK * k + c, BLOCK, stride=2), :]
            yield part, pl.ds(k * BLOCK, BLOCK), pl.ds(c * load, load)

    for k in range(nb):
        c_rs[k].wait()
        for part, rows, cols in halves_of(k):
            q[rows, cols] = part.astype(BF16)
    c_mb.wait()
    pl.semaphore_wait(barrier, len(peers))

    def match(r, k):
        gap = (mb[0, r] - k).astype(F32)
        return jnp.maximum(1.0 - gap * gap, 0.0)

    def exchange(j):
        out = []
        for r in (1, 2, 0):
            block = None
            for k in range(nb):
                part = match(r, k) * q[pl.ds(k * BLOCK, BLOCK), :].astype(F32)
                block = part if block is None else block + part
            ex_send[j, r] = block.astype(BF16)
            out.append(send(ex_send.at[j, r], ex_recv.at[j, r], ex_ss.at[j, r], ex_rs.at[j, r], partners[r], f))
        return out

    def image(j, k):
        top = prod[pl.ds(k * BLOCK, BLOCK), :]
        low = prod[pl.ds(ni + k * BLOCK, BLOCK), :]
        re = top[:, :load] - low[:, load:]
        im = top[:, load:] + low[:, :load]
        if j is not None:
            for r in range(ROUNDS):
                weight = KAPPA * match(r, k)
                inc = ex_recv[j, r].astype(F32)
                re = re - weight * inc[:, :load]
                im = im - weight * inc[:, load:]
        return re, im

    def fold(a):
        return jnp.sum(a.reshape(BLOCK // 8, 8, load), axis=0)

    def pair(v, k):
        rows = pl.ds(k * BLOCK, BLOCK)
        return v[rows, :load], v[rows, load:]

    def inner(a, b):
        return [fold(a[0] * b[0] + a[1] * b[1]), fold(a[0] * b[1] - a[1] * b[0])]

    def total(parts):
        acc = parts[0]
        for p in parts[1:]:
            acc = [i + j for i, j in zip(acc, p)]
        return [jnp.sum(a, axis=0, keepdims=True) for a in acc]

    moves = exchange(0)
    for k in range(nb):
        for part, rows, cols in halves_of(k):
            v0[rows, cols] = part
            qlo[rows, cols] = (part - q[rows, cols].astype(F32)).astype(BF16)
    c_sch.wait()
    prod[...] = jnp.dot(sch[...], qlo[...], preferred_element_type=F32)
    for k in range(nb):
        re, im = image(None, k)
        rows = pl.ds(k * BLOCK, BLOCK)
        u1[rows, :load] = re
        u1[rows, load:] = im
    prod[...] = jnp.dot(sch[...], q[...], preferred_element_type=F32)
    for m in moves:
        m.wait_recv()
    for k in range(nb):
        re, im = image(0, k)
        rows = pl.ds(k * BLOCK, BLOCK)
        v1[rows, :load] = re
        v1[rows, load:] = im
        q[rows, :load] = re.astype(BF16)
        q[rows, load:] = im.astype(BF16)
    moves = exchange(1)
    for k in range(nb):
        rows = pl.ds(k * BLOCK, BLOCK)
        qlo[rows, :] = (v1[rows, :] - q[rows, :].astype(F32)).astype(BF16)
    prod[...] = jnp.dot(sch[...], q[...], preferred_element_type=F32) + jnp.dot(
        sch[...], qlo[...], preferred_element_type=F32
    )
    rows1 = []
    for k in range(nb):
        a = pair(v1, k)
        rows1.append(inner(a, pair(v0, k)) + [fold(abs2(a))])
    rows1 = total(rows1)
    for m in moves:
        m.wait_recv()
    for k in range(nb):
        re, im = image(1, k)
        rows = pl.ds(k * BLOCK, BLOCK)
        v2[rows, :load] = re
        v2[rows, load:] = im
        q[rows, :load] = re.astype(BF16)
        q[rows, load:] = im.astype(BF16)
    moves = exchange(2)
    prod[...] = jnp.dot(sch[...], q[...], preferred_element_type=F32)
    rows2 = []
    for k in range(nb):
        a = pair(v2, k)
        rows2.append(inner(a, pair(v0, k)) + inner(a, pair(v1, k)) + [fold(abs2(a))])
    rows2 = total(rows2)
    for m in moves:
        m.wait_recv()
    rows3 = []
    for k in range(nb):
        a = image(2, k)
        rows3.append(
            inner(a, pair(v0, k)) + inner(a, pair(v1, k)) + inner(a, pair(v2, k)) + [fold(abs2(a))]
        )
    rows3 = total(rows3)

    for i, row in enumerate(rows1 + rows2 + rows3):
        ga_send[i : i + 1, :] = row
    ga_send[15:16, :] = jnp.zeros((1, load), F32)
    moves = [
        send(ga_send, ga_recv.at[i], ga_ss.at[i], ga_rs.at[i], p, f) for i, p in enumerate(group)
    ]
    acc = ga_send[...]
    for i, m in enumerate(moves):
        m.wait_recv()
        acc = acc + ga_recv[i]
    gb_send[...] = acc
    moves = [
        send(gb_send, gb_recv.at[i], gb_ss.at[i], gb_rs.at[i], p, f) for i, p in enumerate(layers)
    ]
    for i, m in enumerate(moves):
        m.wait_recv()
        acc = acc + gb_recv[i]
    row = [acc[i : i + 1, :] for i in range(15)]
    weights = combination((
        (row[0], row[1]), row[2], (row[3], row[4]), (row[5], row[6]), row[7],
        (row[8], row[9]), (row[10], row[11]), (row[12], row[13]), row[14],
    ))
    basis = (v0, v1, u1, v2)

    def solved(start):
        rows = pl.ds(pl.multiple_of(start, PIECE), PIECE)
        re = im = None
        for (wr, wi), v in zip(weights, basis):
            a, b = v[rows, :load], v[rows, load:]
            tr, ti = wr * a - wi * b, wr * b + wi * a
            re, im = (tr, ti) if re is None else (re + tr, im + ti)
        return re, im

    def place(c, half, zt, yt_):
        first = yt_ * (4 * CH) + c * PIECE
        if half == 0:
            return first + (((zt + 1) // 2) % 2) * CH
        return first + 2 * CH + (zt // 2) * CH

    parts, halves, offs = range(PARTS), range(2), range(NY)

    z_moves, y_moves = {}, {}
    for c in parts:
        if c:
            left([z_moves[c - 1, h, off] for h in halves for off in offs])
        for off in (2, 1, 3, 0):
            for h in halves:
                re, im = solved(place(c, h, za[h], yt(off)))
                z1s[c, h, off, :, :load] = re.astype(BF16)
                z1s[c, h, off, :, load:] = im.astype(BF16)
                z_moves[c, h, off] = send(
                    z1s.at[c, h, off], z1r.at[c, h, off], z1_ss.at[c, h, off], z1_rs.at[c, h, off],
                    s, za[h] * NY + yt(off),
                )
    for c in parts:
        for off in (2, 1, 3):
            for h in halves:
                re, im = solved(place(c, h, z, yt(off)))
                y1s[c, h, off - 1, :, :load] = re
                y1s[c, h, off - 1, :, load:] = im
                y_moves[c, h, off] = send(
                    y1s.at[c, h, off - 1], y1r.at[c, h, off - 1], y1_ss.at[c, h, off - 1], y1_rs.at[c, h, off - 1],
                    s, z * NY + yt(off),
                )
    for c in parts:
        for h in halves:
            re, im = solved(place(c, h, z, y))
            own[c, h, :, :load] = re
            own[c, h, :, load:] = im
    c_tbl.wait()

    def sources(c, h):
        out = [(z * NY + y, own.at[c, h])]
        out += [(z * NY + yf(off), y1r.at[c, h, off - 1]) for off in offs[1:]]
        out += [(za[h] * NY + yf(off), z1r.at[c, h, off]) for off in offs]
        return out

    def combine(c, h, zt):
        acc = [None] * NY
        for fs, ref in sources(c, h):
            re, im = ref[:, :load].astype(F32), ref[:, load:].astype(F32)
            for off in offs:
                at = ((zt * NY + yt(off)) * (4 * NY) + fs) * 2
                term = tbl[at] * re + tbl[at + 1] * im
                acc[off] = term if acc[off] is None else acc[off] + term
        return acc

    p_moves = {}

    def pass_on(c, h, slot):
        acc = combine(c, h, opp if slot else za[1 - h])
        for off in offs:
            p2s[c, h, slot, off] = acc[off].astype(BF16)
        p_moves[c, h, slot] = send(
            p2s.at[c, h, slot], p2r.at[c, h, slot], p2_ss.at[c, h, slot], p2_rs.at[c, h, slot],
            s, za[1 - h] * NY + y,
        )

    def hold(c, h, slot):
        acc = combine(c, h, za[h] if slot else z)
        for off in offs:
            keep[c, h, slot, off] = acc[off]

    for c in parts:
        for h in halves:
            for off in offs[1:]:
                y_moves[c, h, off].wait_recv()
            for off in offs:
                z_moves[c, h, off].wait_recv()
            pass_on(c, h, 1)
    left([p_moves[c, h, 1] for c in parts for h in halves])
    for c in parts:
        for h in halves:
            pass_on(c, h, 0)
    for slot in (1, 0):
        for c in parts:
            for h in halves:
                hold(c, h, slot)

    z_moves, y_moves = {}, {}
    for c in parts:
        for h in halves:
            p_moves[c, h, 1].wait_recv()
            for off in (2, 1, 3, 0):
                z3s[c, h, off] = (keep[c, h, 1, off] + p2r[c, h, 1, off].astype(F32)).astype(BF16)
                z_moves[c, h, off] = send(
                    z3s.at[c, h, off], z3r.at[c, h, off], z3_ss.at[c, h, off], z3_rs.at[c, h, off],
                    s, za[h] * NY + yt(off),
                )
    for c in parts:
        for h in halves:
            p_moves[c, h, 0].wait_recv()
            for off in (2, 1, 3):
                y3s[c, h, off - 1] = keep[c, h, 0, off] + p2r[c, h, 0, off].astype(F32)
                y_moves[c, h, off] = send(
                    y3s.at[c, h, off - 1], y3r.at[c, h, off - 1], y3_ss.at[c, h, off - 1], y3_rs.at[c, h, off - 1],
                    s, z * NY + yt(off),
                )
            rows = pl.ds(pl.multiple_of(place(c, h, z, y), PIECE), PIECE)
            out_ref[rows, :] = keep[c, h, 0, 0] + p2r[c, h, 0, 0].astype(F32)
    for c in parts:
        for h in halves:
            for off in offs[1:]:
                y_moves[c, h, off].wait_recv()
                rows = pl.ds(pl.multiple_of(place(c, h, z, yf(off)), PIECE), PIECE)
                out_ref[rows, :] = y3r[c, h, off - 1]
        for h in halves:
            for off in offs:
                z_moves[c, h, off].wait_recv()
                rows = pl.ds(pl.multiple_of(place(c, h, za[h], yf(off)), PIECE), PIECE)
                out_ref[rows, :] = z3r[c, h, off].astype(F32)
    for m in sends:
        m.wait_send()


def shards(right_side, schur, match_blocks):
    ni, _, _, loads = right_side.shape
    freqs = lax.axis_size("freq")
    wide = 2 * loads
    dma = pltpu.SemaphoreType.DMA
    vmem = pltpu.VMEM
    out = pl.pallas_call(
        kernel,
        out_shape=pltpu.VMEM((ni, loads), F32),
        in_specs=[pl.BlockSpec(memory_space=pltpu.HBM)] * 4,
        out_specs=pl.BlockSpec(memory_space=pltpu.VMEM),
        scratch_shapes=[
            pltpu.SMEM((1, ROUNDS), jnp.int32),
            pltpu.SMEM((2 * freqs * freqs,), F32),
            vmem((2 * ni, loads), F32),
            vmem((2 * ni, ni), BF16),
            vmem((ni, wide), F32),
            vmem((ni, wide), F32),
            vmem((ni, wide), F32),
            vmem((ni, wide), F32),
            vmem((ni, wide), BF16),
            vmem((ni, wide), BF16),
            vmem((2 * ni, wide), F32),
            vmem((3, ROUNDS, BLOCK, wide), BF16),
            vmem((3, ROUNDS, BLOCK, wide), BF16),
            vmem((16, loads), F32),
            vmem((7, 16, loads), F32),
            vmem((16, loads), F32),
            vmem((3, 16, loads), F32),
            vmem((PARTS, 2, NY, PIECE, wide), BF16),
            vmem((PARTS, 2, NY, PIECE, wide), BF16),
            vmem((PARTS, 2, NY - 1, PIECE, wide), F32),
            vmem((PARTS, 2, NY - 1, PIECE, wide), F32),
            vmem((PARTS, 2, PIECE, wide), F32),
            vmem((PARTS, 2, 2, NY, PIECE, loads), BF16),
            vmem((PARTS, 2, 2, NY, PIECE, loads), BF16),
            vmem((PARTS, 2, 2, NY, PIECE, loads), F32),
            vmem((PARTS, 2, NY, PIECE, loads), BF16),
            vmem((PARTS, 2, NY, PIECE, loads), BF16),
            vmem((PARTS, 2, NY - 1, PIECE, loads), F32),
            vmem((PARTS, 2, NY - 1, PIECE, loads), F32),
            dma((3 + ni // BLOCK,)),
            dma((3, ROUNDS)), dma((3, ROUNDS)),
            dma((7,)), dma((7,)),
            dma((3,)), dma((3,)),
            dma((PARTS, 2, NY)), dma((PARTS, 2, NY)),
            dma((PARTS, 2, NY - 1)), dma((PARTS, 2, NY - 1)),
            dma((PARTS, 2, 2)), dma((PARTS, 2, 2)),
            dma((PARTS, 2, NY)), dma((PARTS, 2, NY)),
            dma((PARTS, 2, NY - 1)), dma((PARTS, 2, NY - 1)),
        ],
        compiler_params=pltpu.CompilerParams(
            collective_id=0, has_side_effects=True, vmem_limit_bytes=60 * 1024 * 1024
        ),
    )(
        match_blocks,
        jnp.asarray(phase_table(freqs)),
        right_side.reshape(2 * ni, loads),
        schur.reshape(2 * ni, ni),
    )
    return out.reshape(1, ni, loads)


def solution(mesh):
    return jax.shard_map(
        shards,
        mesh=mesh,
        in_specs=(P("sub", "freq", None, None), P("freq", None, "sub", None), P("sub", None)),
        out_specs=P("freq", "sub", None),
        check_vma=False,
    )
```

```python
import jax
import jax.numpy as jnp
import numpy as np
from jax import lax
from jax.experimental import pallas as pl
from jax.experimental.pallas import tpu as pltpu
from jax.sharding import PartitionSpec as P

MESH = pl.DeviceIdType.MESH
F32 = jnp.float32
BF16 = jnp.bfloat16

BLOCK = 128
KAPPA = 0.5
DECAY = 0.5
EPS = 1e-06
ROUNDS = 3
NY = 4
CH = 32
PARTS = 2
PIECE = CH // PARTS


def phase_table(count):
    times = np.arange(count)
    freqs = np.arange(count)
    level = (2 * freqs[None, :] + 1) * times[:, None] % (2 * count)
    angle = np.pi * level / count
    damp = np.exp(DECAY * times / count) / np.sqrt(count)
    table = np.stack([np.cos(angle), -np.sin(angle)], axis=2) * damp[:, None, None]
    return table.astype(np.float32).reshape(-1)


def cmul(a, b):
    return (a[0] * b[0] - a[1] * b[1], a[0] * b[1] + a[1] * b[0])


def conj(a):
    return (a[0], -a[1])


def cadd(a, b):
    return (a[0] + b[0], a[1] + b[1])


def csub(a, b):
    return (a[0] - b[0], a[1] - b[1])


def scale(r, a):
    return (r * a[0], r * a[1])


def abs2(a):
    return a[0] * a[0] + a[1] * a[1]


def divide(a, d):
    return (a[0] / d, a[1] / d)


def combination(g):
    g10, g11, g20, g21, g22, g30, g31, g32, g33 = g
    a0 = divide(g10, g11 + EPS)
    n1 = csub(g10, scale(g11, a0))
    n1 = csub(n1, cmul(conj(a0), g20))
    n1 = cadd(n1, scale(abs2(a0), g21))
    d1 = g11 - 2.0 * cmul(a0, conj(g21))[0] + abs2(a0) * g22
    a1 = divide(n1, jnp.maximum(d1, 0.0) + EPS)
    b = cadd(a0, a1)
    d = cmul(a0, a1)
    n2 = cadd(csub(g10, scale(g11, b)), cmul(d, conj(g21)))
    t = cadd(csub(g20, cmul(b, g21)), scale(g22, d))
    n2 = csub(n2, cmul(conj(b), t))
    t = cadd(csub(g30, cmul(b, g31)), cmul(d, g32))
    n2 = cadd(n2, cmul(conj(d), t))
    d2 = g11 + abs2(b) * g22 + abs2(d) * g33
    d2 = d2 - 2.0 * cmul(b, conj(g21))[0] + 2.0 * cmul(d, conj(g31))[0]
    d2 = d2 - 2.0 * cmul(cmul(conj(b), d), conj(g32))[0]
    a2 = divide(n2, jnp.maximum(d2, 0.0) + EPS)
    w0 = cadd(b, a2)
    w1 = scale(-1.0, cadd(d, cmul(a2, b)))
    wu = scale(-1.0, cmul(a2, a1))
    w2 = cmul(d, a2)
    return w0, w1, wu, w2


def kernel(
    mb_hbm, tbl_hbm, rs_hbm, sch_hbm, out_ref,
    mb, tbl, rs, sch, v0, v1, v2, u1, q, qlo, prod,
    ex_send, ex_recv, ga_send, ga_recv, gb_send, gb_recv,
    z1s, z1r, y1s, y1r, own, p2s, p2r, keep, z3s, z3r, y3s, y3r,
    in_sem, ex_ss, ex_rs, ga_ss, ga_rs, gb_ss, gb_rs,
    z1_ss, z1_rs, y1_ss, y1_rs, p2_ss, p2_rs, z3_ss, z3_rs, y3_ss, y3_rs,
):
    s = lax.axis_index("sub")
    f = lax.axis_index("freq")
    nsub = lax.axis_size("sub")
    z, y = f // NY, f % NY
    ni = v0.shape[0]
    nb = ni // BLOCK
    load = v0.shape[1] // 2

    def flip(bit):
        return s + bit - 2 * bit * ((s // bit) % 2)

    partners = [flip(1), flip(2), flip(8)]
    group = [(s // 8) * 8 + (s + off) % 8 for off in (7, 6, 5, 4, 3, 2, 1)]
    layers = [(s + 8 * off) % nsub for off in range(1, 4)]
    ze = z + 1 - 2 * (z % 2)
    zo = 3 - z
    opp = 3 - ze
    za = (ze, zo)

    def yt(off):
        return (y + off) % NY

    def yf(off):
        return (y + NY - off) % NY

    sends = []

    def left(copies):
        for m in copies:
            m.wait_send()
        sends[:] = [m for m in sends if all(m is not o for o in copies)]


    def send(src, dst, ss, rsem, sub, freq):
        copy = pltpu.make_async_remote_copy(
            src_ref=src, dst_ref=dst, send_sem=ss, recv_sem=rsem,
            device_id={"sub": sub, "freq": freq}, device_id_type=MESH,
        )
        copy.start()
        sends.append(copy)
        return copy

    c_mb = pltpu.make_async_copy(mb_hbm, mb, in_sem.at[0])
    c_tbl = pltpu.make_async_copy(tbl_hbm, tbl, in_sem.at[1])
    c_sch = pltpu.make_async_copy(sch_hbm, sch, in_sem.at[2])
    c_rs = []
    for k in range(nb):
        rows = pl.ds(2 * BLOCK * k, 2 * BLOCK)
        c_rs.append(pltpu.make_async_copy(rs_hbm.at[rows], rs.at[rows], in_sem.at[3 + k]))
    for copy in c_rs + [c_mb, c_sch, c_tbl]:
        copy.start()

    barrier = pltpu.get_barrier_semaphore()
    peers = [(s, zt * NY + yt(off)) for off in (2, 1, 3, 0) for zt in za]
    peers += [(p, f) for p in layers[::-1] + group]
    peers += [(s, z * NY + yt(off)) for off in range(1, NY)]
    for ps, pf in peers:
        pl.semaphore_signal(barrier, inc=1, device_id={"sub": ps, "freq": pf}, device_id_type=MESH)

    def halves_of(k):
        for c in range(2):
            part = rs[pl.ds(2 * BLOCK * k + c, BLOCK, stride=2), :]
            yield part, pl.ds(k * BLOCK, BLOCK), pl.ds(c * load, load)

    for k in range(nb):
        c_rs[k].wait()
        for part, rows, cols in halves_of(k):
            q[rows, cols] = part.astype(BF16)
    c_mb.wait()
    pl.semaphore_wait(barrier, len(peers))

    def match(r, k):
        gap = (mb[0, r] - k).astype(F32)
        return jnp.maximum(1.0 - gap * gap, 0.0)

    def exchange(j):
        out = []
        for r in (1, 2, 0):
            block = None
            for k in range(nb):
                part = match(r, k) * q[pl.ds(k * BLOCK, BLOCK), :].astype(F32)
                block = part if block is None else block + part
            ex_send[j, r] = block.astype(BF16)
            out.append(send(ex_send.at[j, r], ex_recv.at[j, r], ex_ss.at[j, r], ex_rs.at[j, r], partners[r], f))
        return out

    def image(j, k):
        top = prod[pl.ds(k * BLOCK, BLOCK), :]
        low = prod[pl.ds(ni + k * BLOCK, BLOCK), :]
        re = top[:, :load] - low[:, load:]
        im = top[:, load:] + low[:, :load]
        if j is not None:
            for r in range(ROUNDS):
                weight = KAPPA * match(r, k)
                inc = ex_recv[j, r].astype(F32)
                re = re - weight * inc[:, :load]
                im = im - weight * inc[:, load:]
        return re, im

    def fold(a):
        return jnp.sum(a.reshape(BLOCK // 8, 8, load), axis=0)

    def pair(v, k):
        rows = pl.ds(k * BLOCK, BLOCK)
        return v[rows, :load], v[rows, load:]

    def inner(a, b):
        return [fold(a[0] * b[0] + a[1] * b[1]), fold(a[0] * b[1] - a[1] * b[0])]

    def total(parts):
        acc = parts[0]
        for p in parts[1:]:
            acc = [i + j for i, j in zip(acc, p)]
        return [jnp.sum(a, axis=0, keepdims=True) for a in acc]

    moves = exchange(0)
    for k in range(nb):
        for part, rows, cols in halves_of(k):
            v0[rows, cols] = part
            qlo[rows, cols] = (part - q[rows, cols].astype(F32)).astype(BF16)
    c_sch.wait()
    prod[...] = jnp.dot(sch[...], qlo[...], preferred_element_type=F32)
    for k in range(nb):
        re, im = image(None, k)
        rows = pl.ds(k * BLOCK, BLOCK)
        u1[rows, :load] = re
        u1[rows, load:] = im
    prod[...] = jnp.dot(sch[...], q[...], preferred_element_type=F32)
    for m in moves:
        m.wait_recv()
    for k in range(nb):
        re, im = image(0, k)
        rows = pl.ds(k * BLOCK, BLOCK)
        v1[rows, :load] = re
        v1[rows, load:] = im
        q[rows, :load] = re.astype(BF16)
        q[rows, load:] = im.astype(BF16)
    moves = exchange(1)
    for k in range(nb):
        rows = pl.ds(k * BLOCK, BLOCK)
        qlo[rows, :] = (v1[rows, :] - q[rows, :].astype(F32)).astype(BF16)
    prod[...] = jnp.dot(sch[...], q[...], preferred_element_type=F32) + jnp.dot(
        sch[...], qlo[...], preferred_element_type=F32
    )
    rows1 = []
    for k in range(nb):
        a = pair(v1, k)
        rows1.append(inner(a, pair(v0, k)) + [fold(abs2(a))])
    rows1 = total(rows1)
    for m in moves:
        m.wait_recv()
    for k in range(nb):
        re, im = image(1, k)
        rows = pl.ds(k * BLOCK, BLOCK)
        v2[rows, :load] = re
        v2[rows, load:] = im
        q[rows, :load] = re.astype(BF16)
        q[rows, load:] = im.astype(BF16)
    moves = exchange(2)
    prod[...] = jnp.dot(sch[...], q[...], preferred_element_type=F32)
    rows2 = []
    for k in range(nb):
        a = pair(v2, k)
        rows2.append(inner(a, pair(v0, k)) + inner(a, pair(v1, k)) + [fold(abs2(a))])
    rows2 = total(rows2)
    for m in moves:
        m.wait_recv()
    rows3 = []
    for k in range(nb):
        a = image(2, k)
        rows3.append(
            inner(a, pair(v0, k)) + inner(a, pair(v1, k)) + inner(a, pair(v2, k)) + [fold(abs2(a))]
        )
    rows3 = total(rows3)

    for i, row in enumerate(rows1 + rows2 + rows3):
        ga_send[i : i + 1, :] = row
    ga_send[15:16, :] = jnp.zeros((1, load), F32)
    moves = [
        send(ga_send, ga_recv.at[i], ga_ss.at[i], ga_rs.at[i], p, f) for i, p in enumerate(group)
    ]
    acc = ga_send[...]
    for i, m in enumerate(moves):
        m.wait_recv()
        acc = acc + ga_recv[i]
    gb_send[...] = acc
    moves = [
        send(gb_send, gb_recv.at[i], gb_ss.at[i], gb_rs.at[i], p, f) for i, p in enumerate(layers)
    ]
    for i, m in enumerate(moves):
        m.wait_recv()
        acc = acc + gb_recv[i]
    row = [acc[i : i + 1, :] for i in range(15)]
    weights = combination((
        (row[0], row[1]), row[2], (row[3], row[4]), (row[5], row[6]), row[7],
        (row[8], row[9]), (row[10], row[11]), (row[12], row[13]), row[14],
    ))
    basis = (v0, v1, u1, v2)

    def solved(start):
        rows = pl.ds(pl.multiple_of(start, PIECE), PIECE)
        re = im = None
        for (wr, wi), v in zip(weights, basis):
            a, b = v[rows, :load], v[rows, load:]
            tr, ti = wr * a - wi * b, wr * b + wi * a
            re, im = (tr, ti) if re is None else (re + tr, im + ti)
        return re, im

    def place(c, half, zt, yt_):
        first = yt_ * (4 * CH) + c * PIECE
        if half == 0:
            return first + (((zt + 1) // 2) % 2) * CH
        return first + 2 * CH + (zt // 2) * CH

    parts, halves, offs = range(PARTS), range(2), range(NY)

    z_moves, y_moves = {}, {}
    for c in parts:
        if c:
            left([z_moves[c - 1, h, off] for h in halves for off in offs])
        for off in (2, 1, 3, 0):
            for h in halves:
                re, im = solved(place(c, h, za[h], yt(off)))
                z1s[c, h, off, :, :load] = re.astype(BF16)
                z1s[c, h, off, :, load:] = im.astype(BF16)
                z_moves[c, h, off] = send(
                    z1s.at[c, h, off], z1r.at[c, h, off], z1_ss.at[c, h, off], z1_rs.at[c, h, off],
                    s, za[h] * NY + yt(off),
                )
    for c in parts:
        for off in (2, 1, 3):
            for h in halves:
                re, im = solved(place(c, h, z, yt(off)))
                y1s[c, h, off - 1, :, :load] = re
                y1s[c, h, off - 1, :, load:] = im
                y_moves[c, h, off] = send(
                    y1s.at[c, h, off - 1], y1r.at[c, h, off - 1], y1_ss.at[c, h, off - 1], y1_rs.at[c, h, off - 1],
                    s, z * NY + yt(off),
                )
    for c in parts:
        for h in halves:
            re, im = solved(place(c, h, z, y))
            own[c, h, :, :load] = re
            own[c, h, :, load:] = im
    c_tbl.wait()

    def sources(c, h):
        out = [(z * NY + y, own.at[c, h])]
        out += [(z * NY + yf(off), y1r.at[c, h, off - 1]) for off in offs[1:]]
        out += [(za[h] * NY + yf(off), z1r.at[c, h, off]) for off in offs]
        return out

    def combine(c, h, zt):
        acc = [None] * NY
        for fs, ref in sources(c, h):
            re, im = ref[:, :load].astype(F32), ref[:, load:].astype(F32)
            for off in offs:
                at = ((zt * NY + yt(off)) * (4 * NY) + fs) * 2
                term = tbl[at] * re + tbl[at + 1] * im
                acc[off] = term if acc[off] is None else acc[off] + term
        return acc

    p_moves = {}

    def pass_on(c, h, slot):
        acc = combine(c, h, opp if slot else za[1 - h])
        for off in offs:
            p2s[c, h, slot, off] = acc[off].astype(BF16)
        p_moves[c, h, slot] = send(
            p2s.at[c, h, slot], p2r.at[c, h, slot], p2_ss.at[c, h, slot], p2_rs.at[c, h, slot],
            s, za[1 - h] * NY + y,
        )

    def hold(c, h, slot):
        acc = combine(c, h, za[h] if slot else z)
        for off in offs:
            keep[c, h, slot, off] = acc[off]

    for c in parts:
        for h in halves:
            for off in offs[1:]:
                y_moves[c, h, off].wait_recv()
            for off in offs:
                z_moves[c, h, off].wait_recv()
            pass_on(c, h, 1)
    left([p_moves[c, h, 1] for c in parts for h in halves])
    for c in parts:
        if c:
            left([p_moves[c - 1, h, 0] for h in halves])
        for h in halves:
            pass_on(c, h, 0)
    for slot in (1, 0):
        for c in parts:
            for h in halves:
                hold(c, h, slot)

    z_moves, y_moves = {}, {}
    for c in parts:
        for h in halves:
            p_moves[c, h, 1].wait_recv()
            for off in (2, 1, 3, 0):
                z3s[c, h, off] = (keep[c, h, 1, off] + p2r[c, h, 1, off].astype(F32)).astype(BF16)
                z_moves[c, h, off] = send(
                    z3s.at[c, h, off], z3r.at[c, h, off], z3_ss.at[c, h, off], z3_rs.at[c, h, off],
                    s, za[h] * NY + yt(off),
                )
    for c in parts:
        for h in halves:
            p_moves[c, h, 0].wait_recv()
            for off in (2, 1, 3):
                y3s[c, h, off - 1] = keep[c, h, 0, off] + p2r[c, h, 0, off].astype(F32)
                y_moves[c, h, off] = send(
                    y3s.at[c, h, off - 1], y3r.at[c, h, off - 1], y3_ss.at[c, h, off - 1], y3_rs.at[c, h, off - 1],
                    s, z * NY + yt(off),
                )
            rows = pl.ds(pl.multiple_of(place(c, h, z, y), PIECE), PIECE)
            out_ref[rows, :] = keep[c, h, 0, 0] + p2r[c, h, 0, 0].astype(F32)
    for c in parts:
        for h in halves:
            for off in offs[1:]:
                y_moves[c, h, off].wait_recv()
                rows = pl.ds(pl.multiple_of(place(c, h, z, yf(off)), PIECE), PIECE)
                out_ref[rows, :] = y3r[c, h, off - 1]
        for h in halves:
            for off in offs:
                z_moves[c, h, off].wait_recv()
                rows = pl.ds(pl.multiple_of(place(c, h, za[h], yf(off)), PIECE), PIECE)
                out_ref[rows, :] = z3r[c, h, off].astype(F32)
    for m in sends:
        m.wait_send()


def shards(right_side, schur, match_blocks):
    ni, _, _, loads = right_side.shape
    freqs = lax.axis_size("freq")
    wide = 2 * loads
    dma = pltpu.SemaphoreType.DMA
    vmem = pltpu.VMEM
    out = pl.pallas_call(
        kernel,
        out_shape=pltpu.VMEM((ni, loads), F32),
        in_specs=[pl.BlockSpec(memory_space=pltpu.HBM)] * 4,
        out_specs=pl.BlockSpec(memory_space=pltpu.VMEM),
        scratch_shapes=[
            pltpu.SMEM((1, ROUNDS), jnp.int32),
            pltpu.SMEM((2 * freqs * freqs,), F32),
            vmem((2 * ni, loads), F32),
            vmem((2 * ni, ni), BF16),
            vmem((ni, wide), F32),
            vmem((ni, wide), F32),
            vmem((ni, wide), F32),
            vmem((ni, wide), F32),
            vmem((ni, wide), BF16),
            vmem((ni, wide), BF16),
            vmem((2 * ni, wide), F32),
            vmem((3, ROUNDS, BLOCK, wide), BF16),
            vmem((3, ROUNDS, BLOCK, wide), BF16),
            vmem((16, loads), F32),
            vmem((7, 16, loads), F32),
            vmem((16, loads), F32),
            vmem((3, 16, loads), F32),
            vmem((PARTS, 2, NY, PIECE, wide), BF16),
            vmem((PARTS, 2, NY, PIECE, wide), BF16),
            vmem((PARTS, 2, NY - 1, PIECE, wide), F32),
            vmem((PARTS, 2, NY - 1, PIECE, wide), F32),
            vmem((PARTS, 2, PIECE, wide), F32),
            vmem((PARTS, 2, 2, NY, PIECE, loads), BF16),
            vmem((PARTS, 2, 2, NY, PIECE, loads), BF16),
            vmem((PARTS, 2, 2, NY, PIECE, loads), F32),
            vmem((PARTS, 2, NY, PIECE, loads), BF16),
            vmem((PARTS, 2, NY, PIECE, loads), BF16),
            vmem((PARTS, 2, NY - 1, PIECE, loads), F32),
            vmem((PARTS, 2, NY - 1, PIECE, loads), F32),
            dma((3 + ni // BLOCK,)),
            dma((3, ROUNDS)), dma((3, ROUNDS)),
            dma((7,)), dma((7,)),
            dma((3,)), dma((3,)),
            dma((PARTS, 2, NY)), dma((PARTS, 2, NY)),
            dma((PARTS, 2, NY - 1)), dma((PARTS, 2, NY - 1)),
            dma((PARTS, 2, 2)), dma((PARTS, 2, 2)),
            dma((PARTS, 2, NY)), dma((PARTS, 2, NY)),
            dma((PARTS, 2, NY - 1)), dma((PARTS, 2, NY - 1)),
        ],
        compiler_params=pltpu.CompilerParams(
            collective_id=0, has_side_effects=True, vmem_limit_bytes=60 * 1024 * 1024
        ),
    )(
        match_blocks,
        jnp.asarray(phase_table(freqs)),
        right_side.reshape(2 * ni, loads),
        schur.reshape(2 * ni, ni),
    )
    return out.reshape(1, ni, loads)


def solution(mesh):
    return jax.shard_map(
        shards,
        mesh=mesh,
        in_specs=(P("sub", "freq", None, None), P("freq", None, "sub", None), P("sub", None)),
        out_specs=P("freq", "sub", None),
        check_vma=False,
    )
```
